256 devices in a mesh: leaf: 64 (over z, y, core), blk: 4 (over x).
Axes of the slice: x: 4, y: 4, z: 8, core: 2. Of those that a mesh axis runs over, the one named last changes fastest.
Arguments:
- parent_inverse: bfloat16 [64, 512, 512], P('leaf', None, 'blk'), as said below
- leaf_inverse: bfloat16 [896, 512, 512], P('leaf', 'blk'), as said below
- coupling: bfloat16 [896, 512, 512], P('leaf', 'blk'), may hold values from -0.25 to 0.25
- sensitivity: bfloat16 [896, 512, 512], P('leaf', 'blk'), may hold values from -0.25 to 0.25
- parent_of: int32 [896, 1], P('leaf'), may hold values from 0 to 63
- leaf_field: bfloat16 [896, 512], P('leaf'), may hold values from -6 to 6
- parent_field: bfloat16 [64, 512], P('leaf', 'blk'), may hold values from -6 to 6
Outputs:
- leaf_grad: float32 [896, 512], P('leaf', 'blk')
- coupling_grad: float32 [64, 512], P('leaf', 'blk')
The draws below stay inside these ranges and needn't reach their ends.
Inputs may be any that keep to these rules, and one draw needn't show every extreme that they name: `parent_of`: every one of the 64 separator supernodes is the parent of at least one leaf. `parent_inverse`: lower triangular with a positive diagonal. `leaf_inverse`: lower triangular with a positive diagonal.
All inputs are finite; a program needn't handle non-finite values.
Results may differ from the reference program's by a relative error of at most 0.0006.
Values may be sent and summed in bfloat16 or wider, within the bound.
A program may use at most 128 MiB of HBM per device.

```python
import math
import jax
import jax.numpy as jnp
from jax import lax

W = 512
LEAVES = 896
NPAR = 64


def triangle_draw(key, number):
    diag_key, off_key = jax.random.split(key)
    row_index = lax.broadcasted_iota(jnp.int32, (number, W, W), 1)
    col_index = lax.broadcasted_iota(jnp.int32, (number, W, W), 2)
    diagonal = jnp.exp(jax.random.uniform(diag_key, (number, 1, W), jnp.float32, math.log(0.6), math.log(1.6)))
    lower = jax.random.normal(off_key, (number, W, W), jnp.float32) * (0.6 / math.sqrt(W))
    full = jnp.where(row_index > col_index, lower, 0.0) + jnp.where(row_index == col_index, diagonal, 0.0)
    return full.astype(jnp.bfloat16)


def draw_parent_inverse(key, part):
    return triangle_draw(jax.random.fold_in(key, 11), NPAR)


def draw_leaf_inverse(key, part):
    return triangle_draw(jax.random.fold_in(key, 23), LEAVES)


def steps_of(rng, extent, cuts, least, high):
    def one(axis_at, blocks):
        draws = jax.random.uniform(jax.random.fold_in(jax.random.fold_in(rng, 6), axis_at), (blocks,), jnp.float32, least / len(cuts), high / len(cuts))
        return jnp.repeat(jnp.exp(draws), extent[axis_at] // blocks).reshape((-1,) + (1,) * (len(extent) - axis_at - 1))

    gain = one(*cuts[0])
    for cut in cuts[1:]:
        gain = gain * one(*cut)
    return gain


def different_ones(stream_key, rows, count, top, lift):
    ranking = jax.random.permutation(jax.random.fold_in(stream_key, 1), count)
    favour = ranking
    for power in range(3):
        favour = favour * favour // count
    favour = favour * lift // count
    tickets = jax.random.randint(jax.random.fold_in(stream_key, 2), (rows, count), 0, 4096) + favour
    fixed_rows = jax.random.permutation(jax.random.fold_in(stream_key, 3), rows)[jnp.arange(count) % rows]
    tickets = jnp.where(jnp.arange(rows)[:, None] == fixed_rows[None, :], 1 << 14, tickets)
    merit = tickets * count + jnp.arange(count)
    return lax.top_k(merit.astype(jnp.int32), top)[1].astype(jnp.int32)


def scatter_about(stream_key, extent, scale, limit, cuts=(), kind=jnp.bfloat16):
    drawn = scale * jax.random.normal(stream_key, extent, jnp.float32)
    if cuts:
        drawn = drawn * steps_of(stream_key, extent, cuts, -0.22, 0.18)
    return jnp.clip(drawn, -limit, limit).astype(kind)


def setup_inputs(seed: int = 0) -> dict:
    key_of = jax.random.split(jax.random.key(seed), 8)
    return {
        "parent_inverse": draw_parent_inverse(jax.random.fold_in(key_of[7], 71), 0),
        "leaf_inverse": draw_leaf_inverse(jax.random.fold_in(key_of[7], 71), 0),
        "coupling": scatter_about(key_of[2], (LEAVES, W, W), W ** -0.5, 0.25, ((0, 64), (1, 4))),
        "sensitivity": scatter_about(key_of[3], (LEAVES, W, W), W ** -0.5, 0.25, ((0, 64), (1, 4))),
        "parent_of": different_ones(key_of[4], LEAVES, NPAR, 1, 256),
        "leaf_field": scatter_about(key_of[5], (LEAVES, W), 1.0, 6.0, ((0, 64),)),
        "parent_field": scatter_about(key_of[6], (NPAR, W), 1.0, 6.0, ((0, 64), (1, 4))),
    }


def reference(parent_inverse, leaf_inverse, coupling, sensitivity, parent_of, leaf_field, parent_field):
    upper = parent_inverse.astype(jnp.float32)
    parent_cov = jnp.einsum('pki,pkj->pij', upper, upper).astype(jnp.bfloat16)

    def one_leaf(items):
        panel, inverse, sens, field, parent = items
        block = parent_cov[parent[0]]
        above = parent_field[parent[0]].astype(jnp.float32)
        mixed = jnp.dot(panel, inverse, preferred_element_type=jnp.float32).astype(jnp.bfloat16)
        cross = -jnp.dot(block, mixed, preferred_element_type=jnp.float32)
        cross_half = cross.astype(jnp.bfloat16)
        update = jnp.dot(panel.T, cross_half, preferred_element_type=jnp.float32)
        factor = inverse.astype(jnp.float32)
        diagonal = jnp.sum(factor * factor, 0) - jnp.sum(factor * update, 0)
        value = field.astype(jnp.float32)
        leaf_row = 0.5 * (diagonal - value * value)
        returned = jnp.sum(sens.astype(jnp.float32) * cross, 1) - above * jnp.dot(sens, field, preferred_element_type=jnp.float32)
        return leaf_row, returned

    leaf_grad, returned = lax.map(one_leaf, (coupling, leaf_inverse, sensitivity, leaf_field, parent_of))
    owners = (parent_of[:, 0:1] == jnp.arange(NPAR, dtype=jnp.int32)[None, :]).astype(jnp.float32)
    coupling_grad = jnp.dot(owners.T, returned, precision=lax.Precision.HIGHEST, preferred_element_type=jnp.float32)
    return leaf_grad, coupling_grad
```

```python
import jax
import jax.numpy as jnp
from jax import lax
from jax.experimental import pallas as pl
from jax.experimental.pallas import tpu as pltpu
from jax.sharding import PartitionSpec as P

MESH = pl.DeviceIdType.MESH
F32 = jnp.float32
BF16 = jnp.bfloat16
B = 128
W = 512
X, Y, Z = 4, 4, 8
GROUPS = 64
MAXN = 4
EVEN = ((0, 0), (1, 0), (2, 0), (3, 0), (2, 2))
ODD = ((1, 1), (2, 1), (3, 1), (3, 3), (3, 2))
YFIRST = 2


def transposed_dot(a, b):
    return lax.dot_general(a, b, (((0,), (0,)), ((), ())), preferred_element_type=F32)


def at_block(i):
    return pl.ds(pl.multiple_of(i * B, B), B)


def kernel(
    pof, pinv, linv, coup, sens, field, pfield,
    lg_out, cg_out,
    cbuf, lbuf, sbuf, ublk, mixed, mixed_half, crossed, factor, cov, ga, gb, picked,
    fld, masks, fin, got_x, acc, got_all,
    send_p, send_c, send_l, send_s, send_u, send_ring, send_cross, send_f, send_g,
    recv_p, recv_cl, recv_s, recv_u, recv_a, recv_b, recv_cross, recv_f, recv_g,
):
    leaf = lax.axis_index("leaf")
    x = lax.axis_index("blk")
    z = leaf // 8
    y = (leaf // 2) % 4
    c = leaf % 2

    def count(xx):
        return 3 + (xx + c + 1) % 2

    def first(xx):
        return 3 * xx + (xx + 1 - c) // 2

    def plane(d):
        return (x + d) % X

    def remote(src, dst, send, recv, to):
        return pltpu.make_async_remote_copy(src, dst, send, recv, device_id=to, device_id_type=MESH)

    mine = count(x)
    base = first(x)
    counts = [count(plane(d)) for d in range(X)]
    firsts = [first(plane(d)) for d in range(X)]

    def arrived(ref, sem):
        pltpu.make_async_copy(ref, ref, sem).wait()

    barrier = pltpu.get_barrier_semaphore()
    for d in range(1, X):
        pl.semaphore_signal(barrier, inc=1, device_id=(leaf, plane(d)), device_id_type=MESH)

    @pl.loop(1, GROUPS)
    def _(d):
        pl.semaphore_signal(barrier, inc=1, device_id=((leaf + d) % GROUPS, x), device_id_type=MESH)

    zero = jnp.zeros((MAXN, B, B), BF16)
    lbuf[:, 0:B, B : 2 * B] = zero
    lbuf[:, 2 * B : 3 * B, 3 * B : 4 * B] = zero
    factor[0:B, B : 2 * B] = zero[0]
    factor[2 * B : 3 * B, 3 * B : 4 * B] = zero[0]
    fin[...] = jnp.zeros_like(fin)
    pl.semaphore_wait(barrier, X - 1 + GROUPS - 1)

    def slot_a(yy, zz, core=c):
        return core * 32 + zz * 4 + yy

    def slot_b(yy, zz, core=c):
        return core * 32 + yy * 8 + zz

    def own_slot(k):
        return ga.at[slot_a(y, z), k] if k < YFIRST else gb.at[slot_b(y, z), k - YFIRST]

    routes = [(0, k, k) for k in range(4)] + [(1, k, k + 1) for k in range(3)] + [(2, 4, 2), (3, 3, 3)]

    for at in range(X):
        @pl.when(x == at)
        def _(at=at):
            for plane_at, k, rb in routes:
                if plane_at == at:
                    block = pinv.at[0, rb * B : (rb + 1) * B]
                    remote(block, own_slot(k), send_p, recv_p, (leaf, plane(2))).start()
                    pltpu.make_async_copy(block, own_slot(k), recv_p).start()
            if at == 2:
                for d in (1, 3):
                    remote(pinv.at[0, 3 * B :], own_slot(4), send_p, recv_p, (leaf, plane(d))).start()

    def c_copy(d, l):
        return remote(coup.at[firsts[d] + l], cbuf.at[l, at_block(x)], send_c, recv_cl.at[l], (leaf, plane(d)))

    def s_copy(d, l):
        return remote(sens.at[firsts[d] + l], sbuf.at[l, at_block(x)], send_s, recv_s.at[l], (leaf, plane(d)))

    def l_copy(d, l, cb):
        return remote(linv.at[firsts[d] + l, :, at_block(cb)], lbuf.at[l, at_block(x), at_block(cb)],
                      send_l, recv_cl.at[l], (leaf, plane(d)))

    def for_leaf(l, d, fn):
        if l < MAXN - 1:
            fn()
        else:
            pl.when(counts[d] == MAXN)(fn)

    def send_s_panels(leaves):
        for l in leaves:
            for d in (1, 3, 2):
                for_leaf(l, d, lambda l=l, d=d: s_copy(d, l).start())

    for l in range(MAXN):
        for d in (1, 3, 2):
            def send(l=l, d=d):
                c_copy(d, l).start()

                @pl.loop(0, x + 1)
                def _(cb):
                    l_copy(d, l, cb).start()

            for_leaf(l, d, send)
    send_s_panels(range(2))

    @pl.loop(0, mine)
    def _(l):
        pltpu.make_async_copy(coup.at[base + l], cbuf.at[l, at_block(x)], recv_cl.at[l]).start()
        pltpu.make_async_copy(sens.at[base + l], sbuf.at[l, at_block(x)], recv_s.at[l]).start()

        @pl.loop(0, x + 1)
        def _(cb):
            pltpu.make_async_copy(
                linv.at[base + l, :, at_block(cb)], lbuf.at[l, at_block(x), at_block(cb)], recv_cl.at[l]).start()

    def up(n, v, by):
        return (v + by) % n

    def hop(which, ref, along_y, way, sem):
        by = 1 - 2 * way
        to = (z * 8 + up(Y, y, by) * 2 + c, x) if along_y else (up(Z, z, by) * 8 + y * 2 + c, x)
        remote(ref, ref, send_ring.at[which], sem, to).start()

    def a_first(step):
        for way in range(2):
            yy = up(Y, y, -(1 - 2 * way) * (step - 1))
            hop(0, ga.at[slot_a(yy, z)] if step == 1 else ga.at[slot_a(yy, z), way], True, way, recv_a.at[step - 1])

    def a_second(group, step):
        for way in range(2):
            zz = up(Z, z, -(1 - 2 * way) * (step - 1))
            sem = recv_a.at[2 + group * 4 + step - 1]
            if group == 1:
                for side in (way,) if step == 4 else range(2):
                    hop(0, ga.at[slot_a(up(Y, y, 2 * side - 1), zz)], False, way, sem)
            else:
                slot = slot_a(up(Y, y, group), zz)
                hop(0, ga.at[slot, way] if step == 4 else ga.at[slot], False, way, sem)

    def b_first(step):
        for way in range(2):
            slot = slot_b(y, up(Z, z, -(1 - 2 * way) * (step - 1)))
            ref = gb.at[slot, :, way * 64 : way * 64 + 64] if step == 4 else gb.at[slot]
            hop(1, ref, False, way, recv_b.at[step - 1])

    def b_second(group, step):
        for way in range(2):
            yy = up(Y, y, -(1 - 2 * way) * (step - 1))
            sem = recv_b.at[4 + group * 2 + step - 1]
            if group in (0, 4):
                slot = slot_b(yy, up(Z, z, group))
                hop(1, gb.at[slot, :, way * 64 : way * 64 + 64] if step == 2 else gb.at[slot], True, way, sem)
            else:
                for side in (way,) if step == 2 else range(2):
                    hop(1, gb.at[slot_b(yy, up(Z, z, (2 * side - 1) * group))], True, way, sem)

    def across_a(zz):
        ref = ga.at[pl.ds(slot_a(0, zz), 4)]
        remote(ref, ref, send_cross.at[0], recv_cross.at[0], (leaf + 1 - 2 * c, x)).start()

    def across_b(yy):
        ref = gb.at[pl.ds(slot_b(yy, 0), 8)]
        remote(ref, ref, send_cross.at[1], recv_cross.at[1], (leaf + 1 - 2 * c, x)).start()

    def a_first_done(step):
        arrived(ga.at[0 : 2 if step == 1 else 1], recv_a.at[step - 1])
        if step == 1:
            a_first(2)
            a_second(1, 1)
        else:
            a_second(2, 1)
            across_a(z)

    def a_second_done(group, step):
        size = (2 if step == 4 else 4) if group == 1 else (1 if step == 4 else 2)
        arrived(ga.at[0:size], recv_a.at[2 + group * 4 + step - 1])
        if step < 4:
            a_second(group, step + 1)

    def b_first_done(step):
        arrived(gb.at[0 : 1 if step == 4 else 2], recv_b.at[step - 1])
        if step < 4:
            b_first(step + 1)
        b_second(step, 1)
        if step == 4:
            across_b(y)

    def b_second_done(group, step):
        size = (1 if step == 2 else 2) if group in (0, 4) else (2 if step == 2 else 4)
        arrived(gb.at[0:size], recv_b.at[4 + group * 2 + step - 1])
        if step == 1:
            b_second(group, 2)

    arrived(picked.at[0, 0], recv_p)
    b_first(1)
    a_first(1)
    b_second(0, 1)
    a_second(0, 1)
    b_first_done(1)
    a_first_done(1)
    b_second_done(0, 1)
    a_second_done(0, 1)
    b_first_done(2)
    a_first_done(2)
    a_second_done(0, 2)
    b_second_done(1, 1)
    a_second_done(1, 1)
    b_first_done(3)
    a_second_done(2, 1)
    a_second_done(0, 3)
    b_second_done(2, 1)
    a_second_done(1, 2)
    b_first_done(4)
    a_second_done(2, 2)
    for way in range(2):
        across_a(up(Z, z, 2 * way - 1))
    b_second_done(3, 1)
    a_second_done(1, 3)
    a_second_done(2, 3)
    for step in range(2, 4):
        for way in range(2):
            across_a(up(Z, z, (2 * way - 1) * step))
    b_second_done(4, 1)
    for way in range(2):
        across_b(up(Y, y, 2 * way - 1))
    for group in range(3):
        a_second_done(group, 4)
    across_a(up(Z, z, 4))
    for group in range(5):
        b_second_done(group, 2)
    across_b(up(Y, y, 2))
    arrived(ga.at[0:32], recv_cross.at[0])
    arrived(gb.at[0:32], recv_cross.at[1])

    odd = x % 2

    def u_copy(i, l, some):
        ref = picked.at[i, l, pl.ds(0, 4)] if some == 0 else picked.at[i, l, pl.ds(4, 1)]
        dst = ublk.at[l, odd, pl.ds(0, 4)] if some == 0 else ublk.at[l, odd, pl.ds(4, 1)]
        return remote(ref, dst, send_u, recv_u.at[l], (leaf, plane(1 + 2 * i)))

    def chosen(j):
        p = pof[0, j]
        half = (p & 1) * 32
        yy = (p >> 1) & 3
        zz = p >> 3
        a = half + zz * 4 + yy
        b = half + yy * 8 + zz
        return [lambda k=k: ga[a, k] for k in range(YFIRST)] + [lambda k=k: gb[b, k] for k in range(5 - YFIRST)]

    for l in range(MAXN):
        for i in range(2):
            def pick(l=l, i=i):
                block = chosen(firsts[1 + 2 * i] + l)

                @pl.when(x < 2)
                def _():
                    for k in range(4):
                        picked[i, l, k] = block[k]()
                    u_copy(i, l, 0).start()

                @pl.when(x >= 2)
                def _():
                    picked[i, l, 4] = block[4]()
                    u_copy(i, l, 1).start()

            for_leaf(l, 1 + 2 * i, pick)
    send_s_panels(range(2, MAXN))

    for l in range(MAXN):
        def keep(l=l):
            block = chosen(base + l)
            for k in range(5):
                ublk[l, odd, k] = block[k]()

        for_leaf(l, 0, keep)

    fld[0:14] = field[...].astype(F32)
    place = lax.broadcasted_iota(jnp.int32, (GROUPS, B), 0)
    for xx in range(X):
        for l in range(MAXN):
            p = pof[0, jnp.minimum(first(xx) + l, 13)]
            if l == MAXN - 1:
                p = jnp.where(count(xx) == MAXN, p, -1)
            masks[xx * MAXN + l] = jnp.where(place == p, 1.0, 0.0)

    for at, blocks in enumerate((4, 3, 3, 1)):
        @pl.when(x == at)
        def _(blocks=blocks):
            arrived(pinv.at[0, 0 : blocks * B], send_p)
    arrived(ga.at[0:31], send_ring.at[0])
    arrived(gb.at[0:31], send_ring.at[1])
    arrived(ga.at[0:32], send_cross.at[0])
    arrived(gb.at[0:32], send_cross.at[1])

    @pl.loop(0, mine)
    def _(l):
        arrived(ga.at[0:13], recv_cl.at[l])

        left = jnp.dot(cbuf[l], lbuf[l, :, 0 : 2 * B], preferred_element_type=F32)
        mixed[l, :, 0 : 2 * B] = left
        mixed_half[l, :, 0 : 2 * B] = left.astype(BF16)
        right = jnp.dot(cbuf[l, :, 2 * B :], lbuf[l, 2 * B :, 2 * B :], preferred_element_type=F32)
        mixed[l, :, 2 * B :] = right
        mixed_half[l, :, 2 * B :] = right.astype(BF16)
        low = lbuf[l, :, 0 : 2 * B].astype(F32)
        high = lbuf[l, 2 * B :, 2 * B :].astype(F32)
        fin[l, 0:1, 0 : 2 * B] = jnp.sum(low * low, 0, keepdims=True)
        fin[l, 0:1, 2 * B :] = jnp.sum(high * high, 0, keepdims=True)

    @pl.loop(0, mine)
    def _(l):
        arrived(ublk.at[l, 1 - odd], recv_u.at[l])
        for whose, blocks in enumerate((EVEN, ODD)):
            for k, (rb, cb) in enumerate(blocks):
                factor[rb * B : (rb + 1) * B, cb * B : (cb + 1) * B] = ublk[l, whose, k]
        u1 = factor[:, 0 : 2 * B]
        u21 = factor[2 * B :, 0 : 2 * B]
        u2 = factor[2 * B :, 2 * B :]
        cov[0 : 2 * B, 0 : 2 * B] = transposed_dot(u1, u1).astype(BF16)
        cov[0 : 2 * B, 2 * B :] = transposed_dot(u21, u2).astype(BF16)
        cov[2 * B :, 0 : 2 * B] = transposed_dot(u2, u21).astype(BF16)
        cov[2 * B :, 2 * B :] = transposed_dot(u2, u2).astype(BF16)
        total = jnp.zeros((1, W), F32)
        for rb in range(4):
            rows = slice(rb * B, (rb + 1) * B)
            cross = -jnp.dot(cov[rows], mixed_half[l], preferred_element_type=F32)
            crossed[l, rows] = cross
            half = cross.astype(BF16).astype(F32)
            total = total + jnp.sum(half * mixed[l, rows], 0, keepdims=True)
        value = fld[pl.ds(base + l, 1)]
        fin[l, 0:1] = 0.5 * (fin[l, 0:1] - total - value * value)

    for most in range(2):
        @pl.when(mine == 3 + most)
        def _(most=most):
            arrived(coup.at[0 : 11 - most], send_c)
            for at in range(X):
                @pl.when(x == at)
                def _(at=at):
                    arrived(linv.at[0 : 11 - most, :, 0 : (at + 1) * B], send_l)

    @pl.loop(0, mine)
    def _(l):
        arrived(sbuf.at[l], recv_s.at[l])
        value = fld[pl.ds(base + l, 1)].astype(BF16)
        fin[l, 2:3] = lax.dot_general(value, sbuf[l], (((1,), (1,)), ((), ())), preferred_element_type=F32)
        for rb in range(4):
            rows = slice(rb * B, (rb + 1) * B)
            prod = sbuf[l, rows].astype(F32) * crossed[l, rows]
            prod = prod[:, 0:B] + prod[:, B : 2 * B] + prod[:, 2 * B : 3 * B] + prod[:, 3 * B :]
            fin[l, 1:2, rows] = jnp.sum(prod.T, 0, keepdims=True)

    for d in (2, 1, 3):
        remote(fin.at[:, :, at_block(plane(d))], got_x.at[x], send_f, recv_f, (leaf, plane(d))).start()
    got_x[x] = fin[:, :, at_block(x)]
    for most in range(2):
        @pl.when(mine == 3 + most)
        def _(most=most):
            arrived(sens.at[0 : 11 - most], send_s)

            @pl.when(x < 2)
            def _():
                arrived(picked.at[:, 0 : 4 - most, 0:4], send_u)

            @pl.when(x >= 2)
            def _():
                arrived(picked.at[:, 0 : 4 - most, 4:5], send_u)
    arrived(got_x.at[0 : X - 1], recv_f)

    sums = [jnp.zeros((GROUPS, B), F32), jnp.zeros((GROUPS, B), F32)]
    for xx in range(X):
        for l in range(MAXN):
            mask = masks[xx * MAXN + l]
            for q in range(2):
                sums[q] = sums[q] + mask * got_x[xx, l, q + 1 : q + 2]
    for p in range(GROUPS):
        for q in range(2):
            acc[p, q : q + 1] = sums[q][p : p + 1]

    @pl.loop(1, GROUPS)
    def _(d):
        to = (leaf + d) % GROUPS
        remote(acc.at[to], got_all.at[leaf], send_g, recv_g, (to, x)).start()

    got_all[leaf] = acc[leaf]
    arrived(got_x.at[0 : X - 1], send_f)
    for xx in range(X):
        for l in range(MAXN):
            def put(xx=xx, l=l):
                lg_out[pl.ds(first(xx) + l, 1)] = got_x[xx, l, 0:1]

            if l < MAXN - 1:
                put()
            else:
                pl.when(count(xx) == MAXN)(put)
    arrived(got_all.at[0 : GROUPS - 1], recv_g)
    last = jnp.sum(got_all[...], 0)
    cg_out[...] = last[0:1] - pfield[...].astype(F32) * last[1:2]
    arrived(got_all.at[0 : GROUPS - 1], send_g)


def body(parent_inverse, leaf_inverse, coupling, sensitivity, parent_of, leaf_field, parent_field):
    dma = pltpu.SemaphoreType.DMA
    hbm = pl.BlockSpec(memory_space=pltpu.HBM)
    vmem = pl.BlockSpec(memory_space=pltpu.VMEM)
    return pl.pallas_call(
        kernel,
        name="field_gradient",
        out_shape=(jax.ShapeDtypeStruct((14, B), F32), jax.ShapeDtypeStruct((1, B), F32)),
        in_specs=[pl.BlockSpec(memory_space=pltpu.SMEM), hbm, hbm, hbm, hbm, vmem, vmem],
        out_specs=(vmem, vmem),
        scratch_shapes=[
            pltpu.VMEM((MAXN, W, W), BF16),
            pltpu.VMEM((MAXN, W, W), BF16),
            pltpu.VMEM((MAXN, W, W), BF16),
            pltpu.VMEM((MAXN, 2, 5, B, B), BF16),
            pltpu.VMEM((MAXN, W, W), F32),
            pltpu.VMEM((MAXN, W, W), BF16),
            pltpu.VMEM((MAXN, W, W), F32),
            pltpu.VMEM((W, W), BF16),
            pltpu.VMEM((W, W), BF16),
            pltpu.VMEM((GROUPS, YFIRST, B, B), BF16),
            pltpu.VMEM((GROUPS, 5 - YFIRST, B, B), BF16),
            pltpu.VMEM((2, MAXN, 5, B, B), BF16),
            pltpu.VMEM((16, W), F32),
            pltpu.VMEM((X * MAXN, GROUPS, B), F32),
            pltpu.VMEM((MAXN, 4, W), F32),
            pltpu.VMEM((X, MAXN, 4, B), F32),
            pltpu.VMEM((GROUPS, 2, B), F32),
            pltpu.VMEM((GROUPS, 2, B), F32),
            dma, dma, dma, dma, dma, dma((2,)), dma((2,)), dma, dma,
            dma, dma((MAXN,)), dma((MAXN,)), dma((MAXN,)), dma((14,)), dma((14,)), dma((2,)), dma, dma,
        ],
        compiler_params=pltpu.CompilerParams(
            collective_id=0, has_side_effects=True, vmem_limit_bytes=64 * 2**20
        ),
    )(parent_of.reshape(1, 14), parent_inverse, leaf_inverse, coupling, sensitivity, leaf_field, parent_field)


def solution(mesh):
    in_specs = (
        P("leaf", None, "blk"),
        P("leaf", "blk", None),
        P("leaf", "blk", None),
        P("leaf", "blk", None),
        P("leaf", None),
        P("leaf", None),
        P("leaf", "blk"),
    )
    out_specs = (P("leaf", "blk"), P("leaf", "blk"))
    return jax.shard_map(body, mesh=mesh, in_specs=in_specs, out_specs=out_specs, check_vma=False)
```

```python
import jax
import jax.numpy as jnp
from jax import lax
from jax.experimental import pallas as pl
from jax.experimental.pallas import tpu as pltpu
from jax.sharding import PartitionSpec as P

MESH = pl.DeviceIdType.MESH
F32 = jnp.float32
BF16 = jnp.bfloat16
B = 128
W = 512
X, Y, Z = 4, 4, 8
GROUPS = 64
PAIRS = 32
MAXN = 4
EVEN = ((0, 0), (1, 0), (2, 0), (3, 0), (2, 2))
ODD = ((1, 1), (2, 1), (3, 1), (3, 3), (3, 2))
YFIRST = 2


def transposed_dot(a, b):
    return lax.dot_general(a, b, (((0,), (0,)), ((), ())), preferred_element_type=F32)


def at_block(i):
    return pl.ds(pl.multiple_of(i * B, B), B)


def kernel(
    pof, pinv, linv, coup, sens, field, pfield,
    lg_out, cg_out,
    cbuf, lbuf, sbuf, ublk, mixed, mixed_half, crossed, factor, cov, ga, gb, picked,
    vc, vl, vs, fld, fin, got_x, acc, got_all,
    load,
    send_p, send_c, send_l, send_s, send_u, send_ring, send_cross, send_f, send_g,
    recv_p, recv_cl, recv_s, recv_u, recv_a, recv_b, recv_cross, recv_f, recv_g,
):
    leaf = lax.axis_index("leaf")
    x = lax.axis_index("blk")
    z = leaf // 8
    y = (leaf // 2) % 4
    c = leaf % 2

    def count(xx):
        return 3 + (xx + c + 1) % 2

    def first(xx):
        return 3 * xx + (xx + 1 - c) // 2

    def plane(d):
        return (x + d) % X

    def remote(src, dst, send, recv, to):
        return pltpu.make_async_remote_copy(src, dst, send, recv, device_id=to, device_id_type=MESH)

    mine = count(x)
    base = first(x)
    counts = [count(plane(d)) for d in range(X)]
    firsts = [first(plane(d)) for d in range(X)]

    def arrived(ref, sem):
        pltpu.make_async_copy(ref, ref, sem).wait()

    loads = [pltpu.make_async_copy(a, b, load.at[n]) for n, (a, b) in enumerate(((coup, vc), (linv, vl), (sens, vs)))]
    for copy in loads:
        copy.start()

    chip = leaf // 2
    other = leaf + 1 - 2 * c

    def chip_at(n):
        return (chip + (n + 15) % 31 + 1) % PAIRS

    barrier = pltpu.get_barrier_semaphore()

    @pl.loop(0, PAIRS - 1)
    def _(n):
        pl.semaphore_signal(barrier, inc=1, device_id=(chip_at(n) * 2 + c, x), device_id_type=MESH)

    for d in (2, 1, 3):
        pl.semaphore_signal(barrier, inc=1, device_id=(leaf, plane(d)), device_id_type=MESH)
    for d in (2, 1, 3, 0):
        pl.semaphore_signal(barrier, inc=1, device_id=(other, plane(d)), device_id_type=MESH)

    zero = jnp.zeros((MAXN, B, B), BF16)
    lbuf[:, 0:B, B : 2 * B] = zero
    lbuf[:, 2 * B : 3 * B, 3 * B : 4 * B] = zero
    factor[0:B, B : 2 * B] = zero[0]
    factor[2 * B : 3 * B, 3 * B : 4 * B] = zero[0]
    fin[:, 0:3] = jnp.zeros((MAXN, 3, W), F32)
    fin[:, 3:4] = jnp.full((MAXN, 1, W), -1.0, F32)
    pl.semaphore_wait(barrier, PAIRS - 1 + 2 * X - 1)

    def slot_a(yy, zz, core=c):
        return core * 32 + zz * 4 + yy

    def slot_b(yy, zz, core=c):
        return core * 32 + yy * 8 + zz

    def own_slot(k):
        return ga.at[slot_a(y, z), k] if k < YFIRST else gb.at[slot_b(y, z), k - YFIRST]

    routes = [(0, k, k) for k in range(4)] + [(1, k, k + 1) for k in range(3)] + [(2, 4, 2), (3, 3, 3)]

    for at in range(X):
        @pl.when(x == at)
        def _(at=at):
            for plane_at, k, rb in routes:
                if plane_at == at:
                    block = pinv.at[0, rb * B : (rb + 1) * B]
                    remote(block, own_slot(k), send_p, recv_p, (leaf, plane(2))).start()
                    pltpu.make_async_copy(block, own_slot(k), recv_p).start()
            if at == 2:
                for d in (1, 3):
                    remote(pinv.at[0, 3 * B :], own_slot(4), send_p, recv_p, (leaf, plane(d))).start()

    def c_copy(d, l):
        return remote(vc.at[firsts[d] + l], cbuf.at[l, at_block(x)], send_c, recv_cl.at[l], (leaf, plane(d)))

    def s_copy(d, l):
        return remote(vs.at[firsts[d] + l], sbuf.at[l, at_block(x)], send_s, recv_s.at[l], (leaf, plane(d)))

    def l_copy(d, l, cb):
        return remote(vl.at[firsts[d] + l, :, at_block(cb)], lbuf.at[l, at_block(x), at_block(cb)],
                      send_l, recv_cl.at[l], (leaf, plane(d)))

    def for_leaf(l, d, fn):
        if l < MAXN - 1:
            fn()
        else:
            pl.when(counts[d] == MAXN)(fn)

    def send_s_panels(leaves):
        for l in leaves:
            for d in (1, 3, 2):
                for_leaf(l, d, lambda l=l, d=d: s_copy(d, l).start())

    loads[0].wait()
    loads[1].wait()
    for l in range(MAXN):
        for d in (1, 3, 2):
            def send(l=l, d=d):
                c_copy(d, l).start()

                @pl.loop(0, x + 1)
                def _(cb):
                    l_copy(d, l, cb).start()

            for_leaf(l, d, send)
    loads[2].wait()
    send_s_panels(range(2))

    @pl.loop(0, mine)
    def _(l):
        pltpu.make_async_copy(vc.at[base + l], cbuf.at[l, at_block(x)], recv_cl.at[l]).start()
        pltpu.make_async_copy(vs.at[base + l], sbuf.at[l, at_block(x)], recv_s.at[l]).start()

        @pl.loop(0, x + 1)
        def _(cb):
            pltpu.make_async_copy(
                vl.at[base + l, :, at_block(cb)], lbuf.at[l, at_block(x), at_block(cb)], recv_cl.at[l]).start()

    def up(n, v, by):
        return (v + by) % n

    def hop(which, ref, along_y, way, sem):
        by = 1 - 2 * way
        to = (z * 8 + up(Y, y, by) * 2 + c, x) if along_y else (up(Z, z, by) * 8 + y * 2 + c, x)
        remote(ref, ref, send_ring.at[which], sem, to).start()

    def a_first(step):
        for way in range(2):
            yy = up(Y, y, -(1 - 2 * way) * (step - 1))
            hop(0, ga.at[slot_a(yy, z)] if step == 1 else ga.at[slot_a(yy, z), way], True, way, recv_a.at[step - 1])

    def a_second(group, step):
        for way in range(2):
            zz = up(Z, z, -(1 - 2 * way) * (step - 1))
            sem = recv_a.at[2 + group * 4 + step - 1]
            if group == 1:
                for side in (way,) if step == 4 else range(2):
                    hop(0, ga.at[slot_a(up(Y, y, 2 * side - 1), zz)], False, way, sem)
            else:
                slot = slot_a(up(Y, y, group), zz)
                hop(0, ga.at[slot, way] if step == 4 else ga.at[slot], False, way, sem)

    def b_first(step):
        for way in range(2):
            slot = slot_b(y, up(Z, z, -(1 - 2 * way) * (step - 1)))
            ref = gb.at[slot, :, way * 64 : way * 64 + 64] if step == 4 else gb.at[slot]
            hop(1, ref, False, way, recv_b.at[step - 1])

    def b_second(group, step):
        for way in range(2):
            yy = up(Y, y, -(1 - 2 * way) * (step - 1))
            sem = recv_b.at[4 + group * 2 + step - 1]
            if group in (0, 4):
                slot = slot_b(yy, up(Z, z, group))
                hop(1, gb.at[slot, :, way * 64 : way * 64 + 64] if step == 2 else gb.at[slot], True, way, sem)
            else:
                for side in (way,) if step == 2 else range(2):
                    hop(1, gb.at[slot_b(yy, up(Z, z, (2 * side - 1) * group))], True, way, sem)

    def across_a(zz):
        ref = ga.at[pl.ds(slot_a(0, zz), 4)]
        remote(ref, ref, send_cross.at[0], recv_cross.at[0], (leaf + 1 - 2 * c, x)).start()

    def across_b(yy):
        ref = gb.at[pl.ds(slot_b(yy, 0), 8)]
        remote(ref, ref, send_cross.at[1], recv_cross.at[1], (leaf + 1 - 2 * c, x)).start()

    def a_first_done(step):
        arrived(ga.at[0 : 2 if step == 1 else 1], recv_a.at[step - 1])
        if step == 1:
            a_first(2)
            a_second(1, 1)
        else:
            a_second(2, 1)
            across_a(z)

    def a_second_done(group, step):
        size = (2 if step == 4 else 4) if group == 1 else (1 if step == 4 else 2)
        arrived(ga.at[0:size], recv_a.at[2 + group * 4 + step - 1])
        if step < 4:
            a_second(group, step + 1)

    def b_first_done(step):
        arrived(gb.at[0 : 1 if step == 4 else 2], recv_b.at[step - 1])
        if step < 4:
            b_first(step + 1)
        b_second(step, 1)
        if step == 4:
            across_b(y)

    def b_second_done(group, step):
        size = (1 if step == 2 else 2) if group in (0, 4) else (2 if step == 2 else 4)
        arrived(gb.at[0:size], recv_b.at[4 + group * 2 + step - 1])
        if step == 1:
            b_second(group, 2)

    arrived(picked.at[0, 0], recv_p)
    b_first(1)
    a_first(1)
    b_second(0, 1)
    a_second(0, 1)
    b_first_done(1)
    a_first_done(1)
    b_second_done(0, 1)
    a_second_done(0, 1)
    b_first_done(2)
    a_first_done(2)
    a_second_done(0, 2)
    b_second_done(1, 1)
    a_second_done(1, 1)
    b_first_done(3)
    a_second_done(2, 1)
    a_second_done(0, 3)
    b_second_done(2, 1)
    a_second_done(1, 2)
    b_first_done(4)
    a_second_done(2, 2)
    for way in range(2):
        across_a(up(Z, z, 2 * way - 1))
    b_second_done(3, 1)
    a_second_done(1, 3)
    a_second_done(2, 3)
    for step in range(2, 4):
        for way in range(2):
            across_a(up(Z, z, (2 * way - 1) * step))
    b_second_done(4, 1)
    for way in range(2):
        across_b(up(Y, y, 2 * way - 1))
    for group in range(3):
        a_second_done(group, 4)
    across_a(up(Z, z, 4))
    for group in range(5):
        b_second_done(group, 2)
    across_b(up(Y, y, 2))
    arrived(ga.at[0:32], recv_cross.at[0])
    arrived(gb.at[0:32], recv_cross.at[1])

    odd = x % 2

    def u_copy(i, l, some):
        ref = picked.at[i, l, pl.ds(0, 4)] if some == 0 else picked.at[i, l, pl.ds(4, 1)]
        dst = ublk.at[l, odd, pl.ds(0, 4)] if some == 0 else ublk.at[l, odd, pl.ds(4, 1)]
        return remote(ref, dst, send_u, recv_u.at[l], (leaf, plane(1 + 2 * i)))

    def chosen(j):
        p = pof[0, j]
        half = (p & 1) * 32
        yy = (p >> 1) & 3
        zz = p >> 3
        a = half + zz * 4 + yy
        b = half + yy * 8 + zz
        return [lambda k=k: ga[a, k] for k in range(YFIRST)] + [lambda k=k: gb[b, k] for k in range(5 - YFIRST)]

    for l in range(MAXN):
        for i in range(2):
            def pick(l=l, i=i):
                block = chosen(firsts[1 + 2 * i] + l)

                @pl.when(x < 2)
                def _():
                    for k in range(4):
                        picked[i, l, k] = block[k]()
                    u_copy(i, l, 0).start()

                @pl.when(x >= 2)
                def _():
                    picked[i, l, 4] = block[4]()
                    u_copy(i, l, 1).start()

            for_leaf(l, 1 + 2 * i, pick)
    send_s_panels(range(2, MAXN))

    for l in range(MAXN):
        def keep(l=l):
            block = chosen(base + l)
            for k in range(5):
                ublk[l, odd, k] = block[k]()

        for_leaf(l, 0, keep)

    fld[0:14] = field[...].astype(F32)

    @pl.loop(0, mine)
    def _(l):
        fin[l, 3:4] = jnp.full((1, W), pof[0, base + l].astype(F32))

    for at, blocks in enumerate((4, 3, 3, 1)):
        @pl.when(x == at)
        def _(blocks=blocks):
            arrived(pinv.at[0, 0 : blocks * B], send_p)
    arrived(ga.at[0:31], send_ring.at[0])
    arrived(gb.at[0:31], send_ring.at[1])
    arrived(ga.at[0:32], send_cross.at[0])
    arrived(gb.at[0:32], send_cross.at[1])

    @pl.loop(0, mine)
    def _(l):
        arrived(ga.at[0:13], recv_cl.at[l])

        left = jnp.dot(cbuf[l], lbuf[l, :, 0 : 2 * B], preferred_element_type=F32)
        mixed[l, :, 0 : 2 * B] = left
        mixed_half[l, :, 0 : 2 * B] = left.astype(BF16)
        right = jnp.dot(cbuf[l, :, 2 * B :], lbuf[l, 2 * B :, 2 * B :], preferred_element_type=F32)
        mixed[l, :, 2 * B :] = right
        mixed_half[l, :, 2 * B :] = right.astype(BF16)
        low = lbuf[l, :, 0 : 2 * B].astype(F32)
        high = lbuf[l, 2 * B :, 2 * B :].astype(F32)
        fin[l, 0:1, 0 : 2 * B] = jnp.sum(low * low, 0, keepdims=True)
        fin[l, 0:1, 2 * B :] = jnp.sum(high * high, 0, keepdims=True)

    @pl.loop(0, mine)
    def _(l):
        arrived(ublk.at[l, 1 - odd], recv_u.at[l])
        for whose, blocks in enumerate((EVEN, ODD)):
            for k, (rb, cb) in enumerate(blocks):
                factor[rb * B : (rb + 1) * B, cb * B : (cb + 1) * B] = ublk[l, whose, k]
        u1 = factor[:, 0 : 2 * B]
        u21 = factor[2 * B :, 0 : 2 * B]
        u2 = factor[2 * B :, 2 * B :]
        cov[0 : 2 * B, 0 : 2 * B] = transposed_dot(u1, u1).astype(BF16)
        cov[0 : 2 * B, 2 * B :] = transposed_dot(u21, u2).astype(BF16)
        cov[2 * B :, 0 : 2 * B] = transposed_dot(u2, u21).astype(BF16)
        cov[2 * B :, 2 * B :] = transposed_dot(u2, u2).astype(BF16)
        total = jnp.zeros((1, W), F32)
        for rb in range(4):
            rows = slice(rb * B, (rb + 1) * B)
            cross = -jnp.dot(cov[rows], mixed_half[l], preferred_element_type=F32)
            crossed[l, rows] = cross
            half = cross.astype(BF16).astype(F32)
            total = total + jnp.sum(half * mixed[l, rows], 0, keepdims=True)
        value = fld[pl.ds(base + l, 1)]
        fin[l, 0:1] = 0.5 * (fin[l, 0:1] - total - value * value)

    for most in range(2):
        @pl.when(mine == 3 + most)
        def _(most=most):
            arrived(vc.at[0 : 11 - most], send_c)
            for at in range(X):
                @pl.when(x == at)
                def _(at=at):
                    arrived(vl.at[0 : 11 - most, :, 0 : (at + 1) * B], send_l)

    @pl.loop(0, mine)
    def _(l):
        arrived(sbuf.at[l], recv_s.at[l])
        value = fld[pl.ds(base + l, 1)].astype(BF16)
        fin[l, 2:3] = lax.dot_general(value, sbuf[l], (((1,), (1,)), ((), ())), preferred_element_type=F32)
        for rb in range(4):
            rows = slice(rb * B, (rb + 1) * B)
            prod = sbuf[l, rows].astype(F32) * crossed[l, rows]
            prod = prod[:, 0:B] + prod[:, B : 2 * B] + prod[:, 2 * B : 3 * B] + prod[:, 3 * B :]
            fin[l, 1:2, rows] = jnp.sum(prod.T, 0, keepdims=True)

    for d in (2, 1, 3, 0):
        for to in (other, leaf) if d else (other,):
            remote(fin.at[:, :, at_block(plane(d))], got_x.at[c * X + x], send_f, recv_f, (to, plane(d))).start()
    got_x[c * X + x] = fin[:, :, at_block(x)]
    for most in range(2):
        @pl.when(mine == 3 + most)
        def _(most=most):
            arrived(vs.at[0 : 11 - most], send_s)

            @pl.when(x < 2)
            def _():
                arrived(picked.at[:, 0 : 4 - most, 0:4], send_u)

            @pl.when(x >= 2)
            def _():
                arrived(picked.at[:, 0 : 4 - most, 4:5], send_u)
    seven = got_x.at[0 : 2 * X - 1]
    arrived(seven, recv_f)

    place = (lax.broadcasted_iota(jnp.int32, (PAIRS, B), 0) * 2 + c).astype(F32)
    sums = [jnp.zeros((PAIRS, B), F32), jnp.zeros((PAIRS, B), F32)]
    for cc in range(2):
        for xx in range(X):
            for l in range(MAXN):
                rows = got_x[cc * X + xx, l]
                child = place == rows[3:4]
                for q in range(2):
                    sums[q] = sums[q] + jnp.where(child, rows[q + 1 : q + 2], 0.0)
    for p in range(PAIRS):
        for q in range(2):
            acc[p, q : q + 1] = sums[q][p : p + 1]

    @pl.loop(0, PAIRS - 1)
    def _(n):
        to = chip_at(n)
        remote(acc.at[to], got_all.at[chip], send_g, recv_g, (to * 2 + c, x)).start()

    got_all[chip] = acc[chip]
    arrived(seven, send_f)
    for xx in range(X):
        for l in range(MAXN):
            def put(xx=xx, l=l):
                lg_out[pl.ds(first(xx) + l, 1)] = got_x[c * X + xx, l, 0:1]

            if l < MAXN - 1:
                put()
            else:
                pl.when(count(xx) == MAXN)(put)
    arrived(got_all.at[0 : PAIRS - 1], recv_g)
    last = jnp.sum(got_all[...], 0)
    cg_out[...] = last[0:1] - pfield[...].astype(F32) * last[1:2]
    arrived(got_all.at[0 : PAIRS - 1], send_g)


def body(parent_inverse, leaf_inverse, coupling, sensitivity, parent_of, leaf_field, parent_field):
    dma = pltpu.SemaphoreType.DMA
    hbm = pl.BlockSpec(memory_space=pltpu.HBM)
    vmem = pl.BlockSpec(memory_space=pltpu.VMEM)
    return pl.pallas_call(
        kernel,
        name="field_gradient",
        out_shape=(jax.ShapeDtypeStruct((14, B), F32), jax.ShapeDtypeStruct((1, B), F32)),
        in_specs=[pl.BlockSpec(memory_space=pltpu.SMEM), hbm, hbm, hbm, hbm, vmem, vmem],
        out_specs=(vmem, vmem),
        scratch_shapes=[
            pltpu.VMEM((MAXN, W, W), BF16),
            pltpu.VMEM((MAXN, W, W), BF16),
            pltpu.VMEM((MAXN, W, W), BF16),
            pltpu.VMEM((MAXN, 2, 5, B, B), BF16),
            pltpu.VMEM((MAXN, W, W), F32),
            pltpu.VMEM((MAXN, W, W), BF16),
            pltpu.VMEM((MAXN, W, W), F32),
            pltpu.VMEM((W, W), BF16),
            pltpu.VMEM((W, W), BF16),
            pltpu.VMEM((GROUPS, YFIRST, B, B), BF16),
            pltpu.VMEM((GROUPS, 5 - YFIRST, B, B), BF16),
            pltpu.VMEM((2, MAXN, 5, B, B), BF16),
            pltpu.VMEM((14, B, W), BF16),
            pltpu.VMEM((14, B, W), BF16),
            pltpu.VMEM((14, B, W), BF16),
            pltpu.VMEM((16, W), F32),
            pltpu.VMEM((MAXN, 4, W), F32),
            pltpu.VMEM((2 * X, MAXN, 4, B), F32),
            pltpu.VMEM((PAIRS, 2, B), F32),
            pltpu.VMEM((PAIRS, 2, B), F32),
            dma((3,)),
            dma, dma, dma, dma, dma, dma((2,)), dma((2,)), dma, dma,
            dma, dma((MAXN,)), dma((MAXN,)), dma((MAXN,)), dma((14,)), dma((14,)), dma((2,)), dma, dma,
        ],
        compiler_params=pltpu.CompilerParams(
            collective_id=0, has_side_effects=True, vmem_limit_bytes=64 * 2**20
        ),
    )(parent_of.reshape(1, 14), parent_inverse, leaf_inverse, coupling, sensitivity, leaf_field, parent_field)


def solution(mesh):
    in_specs = (
        P("leaf", None, "blk"),
        P("leaf", "blk", None),
        P("leaf", "blk", None),
        P("leaf", "blk", None),
        P("leaf", None),
        P("leaf", None),
        P("leaf", "blk"),
    )
    out_specs = (P("leaf", "blk"), P("leaf", "blk"))
    return jax.shard_map(body, mesh=mesh, in_specs=in_specs, out_specs=out_specs, check_vma=False)
```

```python
import jax
import jax.numpy as jnp
from jax import lax
from jax.experimental import pallas as pl
from jax.experimental.pallas import tpu as pltpu
from jax.sharding import PartitionSpec as P

MESH = pl.DeviceIdType.MESH
F32 = jnp.float32
BF16 = jnp.bfloat16
B = 128
W = 512
X, Y, Z = 4, 4, 8
GROUPS = 64
PAIRS = 32
MAXN = 4
EVEN = ((0, 0), (1, 0), (2, 0), (3, 0), (2, 2))
ODD = ((1, 1), (2, 1), (3, 1), (3, 3), (3, 2))
YFIRST = 2


def transposed_dot(a, b):
    return lax.dot_general(a, b, (((0,), (0,)), ((), ())), preferred_element_type=F32)


def at_block(i):
    return pl.ds(pl.multiple_of(i * B, B), B)


def kernel(
    pof, pinv, linv, coup, sens, field, pfield,
    out,
    cbuf, lbuf, sbuf, ublk, mixed, mixed_half, crossed, factor, cov, ga, gb, picked,
    vc, vl, vs, fld, fin, got_x, acc, got_all,
    load,
    send_p, send_c, send_l, send_s, send_u, send_ring, send_cross, send_f, send_g,
    recv_p, recv_cl, recv_s, recv_u, recv_a, recv_b, recv_cross, recv_f, recv_g,
):
    leaf = lax.axis_index("leaf")
    x = lax.axis_index("blk")
    z = leaf // 8
    y = (leaf // 2) % 4
    c = leaf % 2

    def count(xx):
        return 3 + (xx + c + 1) % 2

    def first(xx):
        return 3 * xx + (xx + 1 - c) // 2

    def plane(d):
        return (x + d) % X

    def remote(src, dst, send, recv, to):
        return pltpu.make_async_remote_copy(src, dst, send, recv, device_id=to, device_id_type=MESH)

    mine = count(x)
    base = first(x)
    counts = [count(plane(d)) for d in range(X)]
    firsts = [first(plane(d)) for d in range(X)]

    def arrived(ref, sem):
        pltpu.make_async_copy(ref, ref, sem).wait()

    loads = [pltpu.make_async_copy(a, b, load.at[n]) for n, (a, b) in enumerate(((coup, vc), (linv, vl), (sens, vs)))]
    for copy in loads:
        copy.start()

    chip = leaf // 2
    other = leaf + 1 - 2 * c

    def chip_at(n):
        return (chip + (n + 15) % 31 + 1) % PAIRS

    barrier = pltpu.get_barrier_semaphore()

    def greet(*to):
        pl.semaphore_signal(barrier, inc=1, device_id=to, device_id_type=MESH)

    for d in (2, 1, 3):
        greet(leaf, plane(d))
    for d in (2, 1, 3, 0):
        greet(other, plane(d))
    for by in (1, -1):
        greet((z + by) % Z * 8 + y * 2 + c, x)
        greet(z * 8 + (y + by) % Y * 2 + c, x)

    zero = jnp.zeros((MAXN, B, B), BF16)
    lbuf[:, 0:B, B : 2 * B] = zero
    lbuf[:, 2 * B : 3 * B, 3 * B : 4 * B] = zero
    factor[0:B, B : 2 * B] = zero[0]
    factor[2 * B : 3 * B, 3 * B : 4 * B] = zero[0]
    fin[:, 0:3] = jnp.zeros((MAXN, 3, W), F32)
    fin[:, 3:4] = jnp.full((MAXN, 1, W), -1.0, F32)
    pl.semaphore_wait(barrier, 2 * X - 1 + 4)

    def slot_a(yy, zz, core=c):
        return core * 32 + zz * 4 + yy

    def slot_b(yy, zz, core=c):
        return core * 32 + yy * 8 + zz

    def own_slot(k):
        return ga.at[slot_a(y, z), k] if k < YFIRST else gb.at[slot_b(y, z), k - YFIRST]

    routes = [(0, k, k) for k in range(4)] + [(1, k, k + 1) for k in range(3)] + [(2, 4, 2), (3, 3, 3)]

    for at in range(X):
        @pl.when(x == at)
        def _(at=at):
            for plane_at, k, rb in routes:
                if plane_at == at:
                    block = pinv.at[0, rb * B : (rb + 1) * B]
                    remote(block, own_slot(k), send_p, recv_p, (leaf, plane(2))).start()
                    pltpu.make_async_copy(block, own_slot(k), recv_p).start()
            if at == 2:
                for d in (1, 3):
                    remote(pinv.at[0, 3 * B :], own_slot(4), send_p, recv_p, (leaf, plane(d))).start()

    def c_copy(d, l):
        return remote((vc if l else coup).at[firsts[d] + l], cbuf.at[l, at_block(x)], send_c, recv_cl.at[l], (leaf, plane(d)))

    def s_copy(d, l):
        return remote(vs.at[firsts[d] + l], sbuf.at[l, at_block(x)], send_s, recv_s.at[l], (leaf, plane(d)))

    def l_copy(d, l, cb):
        return remote((vl if l else linv).at[firsts[d] + l, :, at_block(cb)], lbuf.at[l, at_block(x), at_block(cb)],
                      send_l, recv_cl.at[l], (leaf, plane(d)))

    def for_leaf(l, d, fn):
        if l < MAXN - 1:
            fn()
        else:
            pl.when(counts[d] == MAXN)(fn)

    def send_s_panels(leaves):
        for l in leaves:
            for d in (1, 3, 2):
                for_leaf(l, d, lambda l=l, d=d: s_copy(d, l).start())

    for l in range(MAXN):
        if l == 1:
            loads[0].wait()
            loads[1].wait()
        for d in (1, 3, 2):
            def send(l=l, d=d):
                c_copy(d, l).start()

                @pl.loop(0, x + 1)
                def _(cb):
                    l_copy(d, l, cb).start()

            for_leaf(l, d, send)
    loads[2].wait()
    send_s_panels(range(2))

    @pl.loop(0, mine)
    def _(l):
        pltpu.make_async_copy(vc.at[base + l], cbuf.at[l, at_block(x)], recv_cl.at[l]).start()
        pltpu.make_async_copy(vs.at[base + l], sbuf.at[l, at_block(x)], recv_s.at[l]).start()

        @pl.loop(0, x + 1)
        def _(cb):
            pltpu.make_async_copy(
                vl.at[base + l, :, at_block(cb)], lbuf.at[l, at_block(x), at_block(cb)], recv_cl.at[l]).start()

    def up(n, v, by):
        return (v + by) % n

    def hop(which, ref, along_y, way, sem):
        by = 1 - 2 * way
        to = (z * 8 + up(Y, y, by) * 2 + c, x) if along_y else (up(Z, z, by) * 8 + y * 2 + c, x)
        remote(ref, ref, send_ring.at[which], sem, to).start()

    def a_first(step):
        for way in range(2):
            yy = up(Y, y, -(1 - 2 * way) * (step - 1))
            hop(0, ga.at[slot_a(yy, z)] if step == 1 else ga.at[slot_a(yy, z), way], True, way, recv_a.at[step - 1])

    def a_second(group, step):
        for way in range(2):
            zz = up(Z, z, -(1 - 2 * way) * (step - 1))
            sem = recv_a.at[2 + group * 4 + step - 1]
            if group == 1:
                for side in (way,) if step == 4 else range(2):
                    hop(0, ga.at[slot_a(up(Y, y, 2 * side - 1), zz)], False, way, sem)
            else:
                slot = slot_a(up(Y, y, group), zz)
                hop(0, ga.at[slot, way] if step == 4 else ga.at[slot], False, way, sem)

    def b_first(step):
        for way in range(2):
            slot = slot_b(y, up(Z, z, -(1 - 2 * way) * (step - 1)))
            ref = gb.at[slot, :, way * 64 : way * 64 + 64] if step == 4 else gb.at[slot]
            hop(1, ref, False, way, recv_b.at[step - 1])

    def b_second(group, step):
        for way in range(2):
            yy = up(Y, y, -(1 - 2 * way) * (step - 1))
            sem = recv_b.at[4 + group * 2 + step - 1]
            if group in (0, 4):
                slot = slot_b(yy, up(Z, z, group))
                hop(1, gb.at[slot, :, way * 64 : way * 64 + 64] if step == 2 else gb.at[slot], True, way, sem)
            else:
                for side in (way,) if step == 2 else range(2):
                    hop(1, gb.at[slot_b(yy, up(Z, z, (2 * side - 1) * group))], True, way, sem)

    def across_a(zz):
        ref = ga.at[pl.ds(slot_a(0, zz), 4)]
        remote(ref, ref, send_cross.at[0], recv_cross.at[0], (leaf + 1 - 2 * c, x)).start()

    def across_b(yy):
        ref = gb.at[pl.ds(slot_b(yy, 0), 8)]
        remote(ref, ref, send_cross.at[1], recv_cross.at[1], (leaf + 1 - 2 * c, x)).start()

    def a_first_done(step):
        arrived(ga.at[0 : 2 if step == 1 else 1], recv_a.at[step - 1])
        if step == 1:
            a_first(2)
            a_second(1, 1)
        else:
            a_second(2, 1)
            across_a(z)

    def a_second_done(group, step):
        size = (2 if step == 4 else 4) if group == 1 else (1 if step == 4 else 2)
        arrived(ga.at[0:size], recv_a.at[2 + group * 4 + step - 1])
        if step < 4:
            a_second(group, step + 1)

    def b_first_done(step):
        arrived(gb.at[0 : 1 if step == 4 else 2], recv_b.at[step - 1])
        if step < 4:
            b_first(step + 1)
        b_second(step, 1)
        if step == 4:
            across_b(y)

    def b_second_done(group, step):
        size = (1 if step == 2 else 2) if group in (0, 4) else (2 if step == 2 else 4)
        arrived(gb.at[0:size], recv_b.at[4 + group * 2 + step - 1])
        if step == 1:
            b_second(group, 2)

    arrived(picked.at[0, 0], recv_p)
    b_first(1)
    a_first(1)
    b_second(0, 1)
    a_second(0, 1)
    b_first_done(1)
    a_first_done(1)
    b_second_done(0, 1)
    a_second_done(0, 1)
    b_first_done(2)
    a_first_done(2)
    a_second_done(0, 2)
    b_second_done(1, 1)
    a_second_done(1, 1)
    b_first_done(3)
    a_second_done(2, 1)
    a_second_done(0, 3)
    b_second_done(2, 1)
    a_second_done(1, 2)
    b_first_done(4)
    a_second_done(2, 2)
    for way in range(2):
        across_a(up(Z, z, 2 * way - 1))
    b_second_done(3, 1)
    a_second_done(1, 3)
    a_second_done(2, 3)
    for step in range(2, 4):
        for way in range(2):
            across_a(up(Z, z, (2 * way - 1) * step))
    b_second_done(4, 1)
    for way in range(2):
        across_b(up(Y, y, 2 * way - 1))
    for group in range(3):
        a_second_done(group, 4)
    across_a(up(Z, z, 4))
    for group in range(5):
        b_second_done(group, 2)
    across_b(up(Y, y, 2))
    arrived(ga.at[0:32], recv_cross.at[0])
    arrived(gb.at[0:32], recv_cross.at[1])

    odd = x % 2

    def u_copy(i, l, some):
        ref = picked.at[i, l, pl.ds(0, 4)] if some == 0 else picked.at[i, l, pl.ds(4, 1)]
        dst = ublk.at[l, odd, pl.ds(0, 4)] if some == 0 else ublk.at[l, odd, pl.ds(4, 1)]
        return remote(ref, dst, send_u, recv_u.at[l], (leaf, plane(1 + 2 * i)))

    def chosen(j):
        p = pof[0, j]
        half = (p & 1) * 32
        yy = (p >> 1) & 3
        zz = p >> 3
        a = half + zz * 4 + yy
        b = half + yy * 8 + zz
        return [lambda k=k: ga[a, k] for k in range(YFIRST)] + [lambda k=k: gb[b, k] for k in range(5 - YFIRST)]

    for l in range(MAXN):
        for i in range(2):
            def pick(l=l, i=i):
                block = chosen(firsts[1 + 2 * i] + l)

                @pl.when(x < 2)
                def _():
                    for k in range(4):
                        picked[i, l, k] = block[k]()
                    u_copy(i, l, 0).start()

                @pl.when(x >= 2)
                def _():
                    picked[i, l, 4] = block[4]()
                    u_copy(i, l, 1).start()

            for_leaf(l, 1 + 2 * i, pick)
    send_s_panels(range(2, MAXN))

    for l in range(MAXN):
        def keep(l=l):
            block = chosen(base + l)
            for k in range(5):
                ublk[l, odd, k] = block[k]()

        for_leaf(l, 0, keep)

    fld[0:14] = field[...].astype(F32)

    @pl.loop(0, mine)
    def _(l):
        fin[l, 3:4] = jnp.full((1, W), pof[0, base + l].astype(F32))

    for at, blocks in enumerate((4, 3, 3, 1)):
        @pl.when(x == at)
        def _(blocks=blocks):
            arrived(pinv.at[0, 0 : blocks * B], send_p)
    arrived(ga.at[0:31], send_ring.at[0])
    arrived(gb.at[0:31], send_ring.at[1])
    arrived(ga.at[0:32], send_cross.at[0])
    arrived(gb.at[0:32], send_cross.at[1])

    @pl.loop(0, mine)
    def _(l):
        arrived(ga.at[0:13], recv_cl.at[l])

        left = jnp.dot(cbuf[l], lbuf[l, :, 0 : 2 * B], preferred_element_type=F32)
        mixed[l, :, 0 : 2 * B] = left
        mixed_half[l, :, 0 : 2 * B] = left.astype(BF16)
        right = jnp.dot(cbuf[l, :, 2 * B :], lbuf[l, 2 * B :, 2 * B :], preferred_element_type=F32)
        mixed[l, :, 2 * B :] = right
        mixed_half[l, :, 2 * B :] = right.astype(BF16)
        low = lbuf[l, :, 0 : 2 * B].astype(F32)
        high = lbuf[l, 2 * B :, 2 * B :].astype(F32)
        fin[l, 0:1, 0 : 2 * B] = jnp.sum(low * low, 0, keepdims=True)
        fin[l, 0:1, 2 * B :] = jnp.sum(high * high, 0, keepdims=True)

    @pl.loop(0, mine)
    def _(l):
        arrived(ublk.at[l, 1 - odd], recv_u.at[l])
        for whose, blocks in enumerate((EVEN, ODD)):
            for k, (rb, cb) in enumerate(blocks):
                factor[rb * B : (rb + 1) * B, cb * B : (cb + 1) * B] = ublk[l, whose, k]
        u1 = factor[:, 0 : 2 * B]
        u21 = factor[2 * B :, 0 : 2 * B]
        u2 = factor[2 * B :, 2 * B :]
        cov[0 : 2 * B, 0 : 2 * B] = transposed_dot(u1, u1).astype(BF16)
        cov[0 : 2 * B, 2 * B :] = transposed_dot(u21, u2).astype(BF16)
        cov[2 * B :, 0 : 2 * B] = transposed_dot(u2, u21).astype(BF16)
        cov[2 * B :, 2 * B :] = transposed_dot(u2, u2).astype(BF16)
        total = jnp.zeros((1, W), F32)
        for rb in range(4):
            rows = slice(rb * B, (rb + 1) * B)
            cross = -jnp.dot(cov[rows], mixed_half[l], preferred_element_type=F32)
            crossed[l, rows] = cross
            half = cross.astype(BF16).astype(F32)
            total = total + jnp.sum(half * mixed[l, rows], 0, keepdims=True)
        value = fld[pl.ds(base + l, 1)]
        fin[l, 0:1] = 0.5 * (fin[l, 0:1] - total - value * value)

    for most in range(2):
        @pl.when(mine == 3 + most)
        def _(most=most):
            arrived(vc.at[0 : 11 - most], send_c)
            for at in range(X):
                @pl.when(x == at)
                def _(at=at):
                    arrived(vl.at[0 : 11 - most, :, 0 : (at + 1) * B], send_l)

    @pl.loop(0, mine)
    def _(l):
        arrived(sbuf.at[l], recv_s.at[l])
        value = fld[pl.ds(base + l, 1)].astype(BF16)
        fin[l, 2:3] = lax.dot_general(value, sbuf[l], (((1,), (1,)), ((), ())), preferred_element_type=F32)
        for rb in range(4):
            rows = slice(rb * B, (rb + 1) * B)
            prod = sbuf[l, rows].astype(F32) * crossed[l, rows]
            prod = prod[:, 0:B] + prod[:, B : 2 * B] + prod[:, 2 * B : 3 * B] + prod[:, 3 * B :]
            fin[l, 1:2, rows] = jnp.sum(prod.T, 0, keepdims=True)

    for d in (2, 1, 3, 0):
        for to in (other, leaf) if d else (other,):
            remote(fin.at[:, :, at_block(plane(d))], got_x.at[c * X + x], send_f, recv_f, (to, plane(d))).start()
    got_x[c * X + x] = fin[:, :, at_block(x)]
    for most in range(2):
        @pl.when(mine == 3 + most)
        def _(most=most):
            arrived(vs.at[0 : 11 - most], send_s)

            @pl.when(x < 2)
            def _():
                arrived(picked.at[:, 0 : 4 - most, 0:4], send_u)

            @pl.when(x >= 2)
            def _():
                arrived(picked.at[:, 0 : 4 - most, 4:5], send_u)
    seven = got_x.at[0 : 2 * X - 1]
    arrived(seven, recv_f)

    place = (lax.broadcasted_iota(jnp.int32, (PAIRS, B), 0) * 2 + c).astype(F32)
    sums = [jnp.zeros((PAIRS, B), F32), jnp.zeros((PAIRS, B), F32)]
    for cc in range(2):
        for xx in range(X):
            for l in range(MAXN):
                rows = got_x[cc * X + xx, l]
                child = place == rows[3:4]
                for q in range(2):
                    sums[q] = sums[q] + jnp.where(child, rows[q + 1 : q + 2], 0.0)
    for p in range(PAIRS):
        for q in range(2):
            acc[p, q : q + 1] = sums[q][p : p + 1]

    @pl.loop(0, PAIRS - 1)
    def _(n):
        to = chip_at(n)
        remote(acc.at[to], got_all.at[chip], send_g, recv_g, (to * 2 + c, x)).start()

    got_all[chip] = acc[chip]
    arrived(seven, send_f)
    for xx in range(X):
        for l in range(MAXN):
            def put(xx=xx, l=l):
                out[pl.ds(first(xx) + l, 1)] = got_x[c * X + xx, l, 0:1]

            if l < MAXN - 1:
                put()
            else:
                pl.when(count(xx) == MAXN)(put)
    arrived(got_all.at[0 : PAIRS - 1], recv_g)
    last = jnp.sum(got_all[...], 0)
    out[14:15] = last[0:1] - pfield[...].astype(F32) * last[1:2]
    arrived(got_all.at[0 : PAIRS - 1], send_g)


def split_rows(rows, leaf_grad, coupling_grad):
    leaf_grad[...] = rows[0:14]
    coupling_grad[...] = rows[14:15]


def body(parent_inverse, leaf_inverse, coupling, sensitivity, parent_of, leaf_field, parent_field):
    dma = pltpu.SemaphoreType.DMA
    hbm = pl.BlockSpec(memory_space=pltpu.HBM)
    vmem = pl.BlockSpec(memory_space=pltpu.VMEM)
    rows = pl.pallas_call(
        kernel,
        name="field_gradient",
        out_shape=jax.ShapeDtypeStruct((16, B), F32),
        in_specs=[pl.BlockSpec(memory_space=pltpu.SMEM), hbm, hbm, hbm, hbm, vmem, vmem],
        out_specs=vmem,
        scratch_shapes=[
            pltpu.VMEM((MAXN, W, W), BF16),
            pltpu.VMEM((MAXN, W, W), BF16),
            pltpu.VMEM((MAXN, W, W), BF16),
            pltpu.VMEM((MAXN, 2, 5, B, B), BF16),
            pltpu.VMEM((MAXN, W, W), F32),
            pltpu.VMEM((MAXN, W, W), BF16),
            pltpu.VMEM((MAXN, W, W), F32),
            pltpu.VMEM((W, W), BF16),
            pltpu.VMEM((W, W), BF16),
            pltpu.VMEM((GROUPS, YFIRST, B, B), BF16),
            pltpu.VMEM((GROUPS, 5 - YFIRST, B, B), BF16),
            pltpu.VMEM((2, MAXN, 5, B, B), BF16),
            pltpu.VMEM((14, B, W), BF16),
            pltpu.VMEM((14, B, W), BF16),
            pltpu.VMEM((14, B, W), BF16),
            pltpu.VMEM((16, W), F32),
            pltpu.VMEM((MAXN, 4, W), F32),
            pltpu.VMEM((2 * X, MAXN, 4, B), F32),
            pltpu.VMEM((PAIRS, 2, B), F32),
            pltpu.VMEM((PAIRS, 2, B), F32),
            dma((3,)),
            dma, dma, dma, dma, dma, dma((2,)), dma((2,)), dma, dma,
            dma, dma((MAXN,)), dma((MAXN,)), dma((MAXN,)), dma((14,)), dma((14,)), dma((2,)), dma, dma,
        ],
        compiler_params=pltpu.CompilerParams(
            collective_id=0, has_side_effects=True, vmem_limit_bytes=64 * 2**20
        ),
    )(parent_of.reshape(1, 14), parent_inverse, leaf_inverse, coupling, sensitivity, leaf_field, parent_field)
    return pl.pallas_call(
        split_rows,
        name="split_rows",
        out_shape=(jax.ShapeDtypeStruct((14, B), F32), jax.ShapeDtypeStruct((1, B), F32)),
        in_specs=[vmem],
        out_specs=(vmem, vmem),
    )(rows)


def solution(mesh):
    in_specs = (
        P("leaf", None, "blk"),
        P("leaf", "blk", None),
        P("leaf", "blk", None),
        P("leaf", "blk", None),
        P("leaf", None),
        P("leaf", None),
        P("leaf", "blk"),
    )
    out_specs = (P("leaf", "blk"), P("leaf", "blk"))
    return jax.shard_map(body, mesh=mesh, in_specs=in_specs, out_specs=out_specs, check_vma=False)
```

```python
import jax
import jax.numpy as jnp
from jax import lax
from jax.experimental import pallas as pl
from jax.experimental.pallas import tpu as pltpu
from jax.sharding import PartitionSpec as P

MESH = pl.DeviceIdType.MESH
F32 = jnp.float32
BF16 = jnp.bfloat16
B = 128
W = 512
X, Y, Z = 4, 4, 8
GROUPS = 64
PAIRS = 32
MAXN = 4
EVEN = ((0, 0), (1, 0), (2, 0), (3, 0), (2, 2))
ODD = ((1, 1), (2, 1), (3, 1), (3, 3), (3, 2))
YFIRST = 2

BELOW = (1, 4, 5, 1)


def shares():
    table = {}
    for d, n in enumerate(BELOW):
        table[(d - 1) % X, 0] = (0, n) if n > 2 else (5 - n, 5)
        table[(d + 1) % X, 1] = (n, 5) if n > 2 else (0, 5 - n)
    return table


SHARES = shares()
EARLY = 2


def transposed_dot(a, b):
    return lax.dot_general(a, b, (((0,), (0,)), ((), ())), preferred_element_type=F32)


def at_block(i):
    return pl.ds(pl.multiple_of(i * B, B), B)


def kernel(
    pof, pinv, linv, coup, sens, field, pfield,
    out,
    cbuf, lbuf, sbuf, ublk, mixed, mixed_half, crossed, factor, cov, ga, gb, picked,
    vc, vl, vs, fld, fin, got_x, acc, got_all,
    load,
    send_p, send_c, send_l, send_s, send_u, send_ring, send_cross, send_f, send_g,
    recv_p, recv_cl, recv_s, recv_u, recv_a, recv_b, recv_cross, recv_f, recv_g,
):
    leaf = lax.axis_index("leaf")
    x = lax.axis_index("blk")
    z = leaf // 8
    y = (leaf // 2) % 4
    c = leaf % 2

    def count(xx):
        return 3 + (xx + c + 1) % 2

    def first(xx):
        return 3 * xx + (xx + 1 - c) // 2

    def plane(d):
        return (x + d) % X

    def remote(src, dst, send, recv, to):
        return pltpu.make_async_remote_copy(src, dst, send, recv, device_id=to, device_id_type=MESH)

    mine = count(x)
    base = first(x)
    counts = [count(plane(d)) for d in range(X)]
    firsts = [first(plane(d)) for d in range(X)]

    def arrived(ref, sem):
        pltpu.make_async_copy(ref, ref, sem).wait()

    loads = [pltpu.make_async_copy(a, b, load.at[n]) for n, (a, b) in enumerate(((coup, vc), (linv, vl), (sens, vs)))]
    for copy in loads:
        copy.start()

    chip = leaf // 2
    other = leaf + 1 - 2 * c

    def chip_at(n):
        return (chip + (n + 15) % 31 + 1) % PAIRS

    barrier = pltpu.get_barrier_semaphore()

    def greet(*to):
        pl.semaphore_signal(barrier, inc=1, device_id=to, device_id_type=MESH)

    for d in (2, 1, 3):
        greet(leaf, plane(d))
    for d in (2, 1, 3, 0):
        greet(other, plane(d))
    for by in (1, -1):
        greet((z + by) % Z * 8 + y * 2 + c, x)
        greet(z * 8 + (y + by) % Y * 2 + c, x)

    zero = jnp.zeros((MAXN, B, B), BF16)
    lbuf[:, 0:B, B : 2 * B] = zero
    lbuf[:, 2 * B : 3 * B, 3 * B : 4 * B] = zero
    factor[0:B, B : 2 * B] = zero[0]
    factor[2 * B : 3 * B, 3 * B : 4 * B] = zero[0]
    fin[:, 0:3] = jnp.zeros((MAXN, 3, W), F32)
    fin[:, 3:4] = jnp.full((MAXN, 1, W), -1.0, F32)
    pl.semaphore_wait(barrier, 2 * X - 1 + 4)

    def slot_a(yy, zz, core=c):
        return core * 32 + zz * 4 + yy

    def slot_b(yy, zz, core=c):
        return core * 32 + yy * 8 + zz

    def own_slot(k):
        return ga.at[slot_a(y, z), k] if k < YFIRST else gb.at[slot_b(y, z), k - YFIRST]

    routes = [(0, k, k) for k in range(4)] + [(1, k, k + 1) for k in range(3)] + [(2, 4, 2), (3, 3, 3)]

    for at in range(X):
        @pl.when(x == at)
        def _(at=at):
            for plane_at, k, rb in routes:
                if plane_at == at:
                    block = pinv.at[0, rb * B : (rb + 1) * B]
                    remote(block, own_slot(k), send_p, recv_p, (leaf, plane(2))).start()
                    pltpu.make_async_copy(block, own_slot(k), recv_p).start()
            if at == 2:
                for d in (1, 3):
                    remote(pinv.at[0, 3 * B :], own_slot(4), send_p, recv_p, (leaf, plane(d))).start()

    def c_copy(d, l):
        return remote((vc if l else coup).at[firsts[d] + l], cbuf.at[l, at_block(x)], send_c, recv_cl.at[l], (leaf, plane(d)))

    def s_copy(d, l):
        return remote(vs.at[firsts[d] + l], sbuf.at[l, at_block(x)], send_s, recv_s.at[l], (leaf, plane(d)))

    def l_copy(d, l, cb):
        return remote((vl if l else linv).at[firsts[d] + l, :, at_block(cb)], lbuf.at[l, at_block(x), at_block(cb)],
                      send_l, recv_cl.at[l], (leaf, plane(d)))

    def for_leaf(l, d, fn):
        if l < MAXN - 1:
            fn()
        else:
            pl.when(counts[d] == MAXN)(fn)

    def send_s_panels(leaves):
        for l in leaves:
            for d in (1, 3, 2):
                for_leaf(l, d, lambda l=l, d=d: s_copy(d, l).start())

    for l in range(MAXN):
        if l == 1:
            loads[0].wait()
            loads[1].wait()
        for d in (1, 3, 2):
            def send(l=l, d=d):
                c_copy(d, l).start()

                @pl.loop(0, x + 1)
                def _(cb):
                    l_copy(d, l, cb).start()

            for_leaf(l, d, send)
    loads[2].wait()
    send_s_panels(range(EARLY))

    @pl.loop(0, mine)
    def _(l):
        pltpu.make_async_copy(vc.at[base + l], cbuf.at[l, at_block(x)], recv_cl.at[l]).start()
        pltpu.make_async_copy(vs.at[base + l], sbuf.at[l, at_block(x)], recv_s.at[l]).start()

        @pl.loop(0, x + 1)
        def _(cb):
            pltpu.make_async_copy(
                vl.at[base + l, :, at_block(cb)], lbuf.at[l, at_block(x), at_block(cb)], recv_cl.at[l]).start()

    def up(n, v, by):
        return (v + by) % n

    def hop(which, ref, along_y, way, sem):
        by = 1 - 2 * way
        to = (z * 8 + up(Y, y, by) * 2 + c, x) if along_y else (up(Z, z, by) * 8 + y * 2 + c, x)
        remote(ref, ref, send_ring.at[which], sem, to).start()

    def a_first(step):
        for way in range(2):
            yy = up(Y, y, -(1 - 2 * way) * (step - 1))
            hop(0, ga.at[slot_a(yy, z)] if step == 1 else ga.at[slot_a(yy, z), way], True, way, recv_a.at[step - 1])

    def a_second(group, step):
        for way in range(2):
            zz = up(Z, z, -(1 - 2 * way) * (step - 1))
            sem = recv_a.at[2 + group * 4 + step - 1]
            if group == 1:
                for side in (way,) if step == 4 else range(2):
                    hop(0, ga.at[slot_a(up(Y, y, 2 * side - 1), zz)], False, way, sem)
            else:
                slot = slot_a(up(Y, y, group), zz)
                hop(0, ga.at[slot, way] if step == 4 else ga.at[slot], False, way, sem)

    def b_first(step):
        for way in range(2):
            slot = slot_b(y, up(Z, z, -(1 - 2 * way) * (step - 1)))
            ref = gb.at[slot, :, way * 64 : way * 64 + 64] if step == 4 else gb.at[slot]
            hop(1, ref, False, way, recv_b.at[step - 1])

    def b_second(group, step):
        for way in range(2):
            yy = up(Y, y, -(1 - 2 * way) * (step - 1))
            sem = recv_b.at[4 + group * 2 + step - 1]
            if group in (0, 4):
                slot = slot_b(yy, up(Z, z, group))
                hop(1, gb.at[slot, :, way * 64 : way * 64 + 64] if step == 2 else gb.at[slot], True, way, sem)
            else:
                for side in (way,) if step == 2 else range(2):
                    hop(1, gb.at[slot_b(yy, up(Z, z, (2 * side - 1) * group))], True, way, sem)

    def across_a(zz):
        ref = ga.at[pl.ds(slot_a(0, zz), 4)]
        remote(ref, ref, send_cross.at[0], recv_cross.at[0], (leaf + 1 - 2 * c, x)).start()

    def across_b(yy):
        ref = gb.at[pl.ds(slot_b(yy, 0), 8)]
        remote(ref, ref, send_cross.at[1], recv_cross.at[1], (leaf + 1 - 2 * c, x)).start()

    def a_first_done(step):
        arrived(ga.at[0 : 2 if step == 1 else 1], recv_a.at[step - 1])
        if step == 1:
            a_first(2)
            a_second(1, 1)
        else:
            a_second(2, 1)
            across_a(z)

    def a_second_done(group, step):
        size = (2 if step == 4 else 4) if group == 1 else (1 if step == 4 else 2)
        arrived(ga.at[0:size], recv_a.at[2 + group * 4 + step - 1])
        if step < 4:
            a_second(group, step + 1)

    def b_first_done(step):
        arrived(gb.at[0 : 1 if step == 4 else 2], recv_b.at[step - 1])
        if step < 4:
            b_first(step + 1)
        b_second(step, 1)
        if step == 4:
            across_b(y)

    def b_second_done(group, step):
        size = (1 if step == 2 else 2) if group in (0, 4) else (2 if step == 2 else 4)
        arrived(gb.at[0:size], recv_b.at[4 + group * 2 + step - 1])
        if step == 1:
            b_second(group, 2)

    arrived(picked.at[0, 0], recv_p)
    b_first(1)
    a_first(1)
    b_second(0, 1)
    a_second(0, 1)
    b_first_done(1)
    a_first_done(1)
    b_second_done(0, 1)
    a_second_done(0, 1)
    b_first_done(2)
    a_first_done(2)
    a_second_done(0, 2)
    b_second_done(1, 1)
    a_second_done(1, 1)
    b_first_done(3)
    a_second_done(2, 1)
    a_second_done(0, 3)
    b_second_done(2, 1)
    a_second_done(1, 2)
    b_first_done(4)
    a_second_done(2, 2)
    for way in range(2):
        across_a(up(Z, z, 2 * way - 1))
    b_second_done(3, 1)
    a_second_done(1, 3)
    a_second_done(2, 3)
    for step in range(2, 4):
        for way in range(2):
            across_a(up(Z, z, (2 * way - 1) * step))
    b_second_done(4, 1)
    for way in range(2):
        across_b(up(Y, y, 2 * way - 1))
    for group in range(3):
        a_second_done(group, 4)
    across_a(up(Z, z, 4))
    for group in range(5):
        b_second_done(group, 2)
    across_b(up(Y, y, 2))
    arrived(ga.at[0:32], recv_cross.at[0])
    arrived(gb.at[0:32], recv_cross.at[1])

    odd = x % 2

    def u_copy(i, l, low, high):
        return remote(picked.at[i, l, pl.ds(low, high - low)], ublk.at[l, odd, pl.ds(low, high - low)],
                      send_u, recv_u.at[l], (leaf, plane(1 + 2 * i)))

    def chosen(j):
        p = pof[0, j]
        half = (p & 1) * 32
        yy = (p >> 1) & 3
        zz = p >> 3
        a = half + zz * 4 + yy
        b = half + yy * 8 + zz
        return [lambda k=k: ga[a, k] for k in range(YFIRST)] + [lambda k=k: gb[b, k] for k in range(5 - YFIRST)]

    for l in range(MAXN):
        for i in range(2):
            def pick(l=l, i=i):
                block = chosen(firsts[1 + 2 * i] + l)

                for (at, way), (low, high) in SHARES.items():
                    if way == i and high > low:
                        @pl.when(x == at)
                        def _(low=low, high=high):
                            for k in range(low, high):
                                picked[i, l, k] = block[k]()
                            u_copy(i, l, low, high).start()

            for_leaf(l, 1 + 2 * i, pick)
    send_s_panels(range(EARLY, MAXN))

    for l in range(MAXN):
        def keep(l=l):
            block = chosen(base + l)
            for k in range(5):
                ublk[l, odd, k] = block[k]()

        for_leaf(l, 0, keep)

    fld[0:14] = field[...].astype(F32)

    @pl.loop(0, mine)
    def _(l):
        fin[l, 3:4] = jnp.full((1, W), pof[0, base + l].astype(F32))

    for at, blocks in enumerate((4, 3, 3, 1)):
        @pl.when(x == at)
        def _(blocks=blocks):
            arrived(pinv.at[0, 0 : blocks * B], send_p)
    arrived(ga.at[0:31], send_ring.at[0])
    arrived(gb.at[0:31], send_ring.at[1])
    arrived(ga.at[0:32], send_cross.at[0])
    arrived(gb.at[0:32], send_cross.at[1])

    @pl.loop(0, mine)
    def _(l):
        arrived(ga.at[0:13], recv_cl.at[l])

        left = jnp.dot(cbuf[l], lbuf[l, :, 0 : 2 * B], preferred_element_type=F32)
        mixed[l, :, 0 : 2 * B] = left
        mixed_half[l, :, 0 : 2 * B] = left.astype(BF16)
        right = jnp.dot(cbuf[l, :, 2 * B :], lbuf[l, 2 * B :, 2 * B :], preferred_element_type=F32)
        mixed[l, :, 2 * B :] = right
        mixed_half[l, :, 2 * B :] = right.astype(BF16)
        low = lbuf[l, :, 0 : 2 * B].astype(F32)
        high = lbuf[l, 2 * B :, 2 * B :].astype(F32)
        fin[l, 0:1, 0 : 2 * B] = jnp.sum(low * low, 0, keepdims=True)
        fin[l, 0:1, 2 * B :] = jnp.sum(high * high, 0, keepdims=True)

    @pl.loop(0, mine)
    def _(l):
        arrived(ublk.at[l, 1 - odd], recv_u.at[l])
        for whose, blocks in enumerate((EVEN, ODD)):
            for k, (rb, cb) in enumerate(blocks):
                factor[rb * B : (rb + 1) * B, cb * B : (cb + 1) * B] = ublk[l, whose, k]
        u1 = factor[:, 0 : 2 * B]
        u21 = factor[2 * B :, 0 : 2 * B]
        u2 = factor[2 * B :, 2 * B :]
        cov[0 : 2 * B, 0 : 2 * B] = transposed_dot(u1, u1).astype(BF16)
        cov[0 : 2 * B, 2 * B :] = transposed_dot(u21, u2).astype(BF16)
        cov[2 * B :, 0 : 2 * B] = transposed_dot(u2, u21).astype(BF16)
        cov[2 * B :, 2 * B :] = transposed_dot(u2, u2).astype(BF16)
        total = jnp.zeros((1, W), F32)
        for rb in range(4):
            rows = slice(rb * B, (rb + 1) * B)
            cross = -jnp.dot(cov[rows], mixed_half[l], preferred_element_type=F32)
            crossed[l, rows] = cross
            half = cross.astype(BF16).astype(F32)
            total = total + jnp.sum(half * mixed[l, rows], 0, keepdims=True)
        value = fld[pl.ds(base + l, 1)]
        fin[l, 0:1] = 0.5 * (fin[l, 0:1] - total - value * value)

    for most in range(2):
        @pl.when(mine == 3 + most)
        def _(most=most):
            arrived(vc.at[0 : 11 - most], send_c)
            for at in range(X):
                @pl.when(x == at)
                def _(at=at):
                    arrived(vl.at[0 : 11 - most, :, 0 : (at + 1) * B], send_l)

    @pl.loop(0, mine)
    def _(l):
        arrived(sbuf.at[l], recv_s.at[l])
        value = fld[pl.ds(base + l, 1)].astype(BF16)
        fin[l, 2:3] = lax.dot_general(value, sbuf[l], (((1,), (1,)), ((), ())), preferred_element_type=F32)
        for rb in range(4):
            rows = slice(rb * B, (rb + 1) * B)
            prod = sbuf[l, rows].astype(F32) * crossed[l, rows]
            prod = prod[:, 0:B] + prod[:, B : 2 * B] + prod[:, 2 * B : 3 * B] + prod[:, 3 * B :]
            fin[l, 1:2, rows] = jnp.sum(prod.T, 0, keepdims=True)

    for d in (2, 1, 3, 0):
        for to in (other, leaf) if d else (other,):
            remote(fin.at[:, :, at_block(plane(d))], got_x.at[c * X + x], send_f, recv_f, (to, plane(d))).start()
    got_x[c * X + x] = fin[:, :, at_block(x)]
    for most in range(2):
        @pl.when(mine == 3 + most)
        def _(most=most):
            arrived(vs.at[0 : 11 - most], send_s)

            for (at, way), (low, high) in SHARES.items():
                if high > low:
                    @pl.when(x == at)
                    def _(way=way, low=low, high=high):
                        arrived(picked.at[way, 0 : 4 - most, low:high], send_u)
    seven = got_x.at[0 : 2 * X - 1]
    arrived(seven, recv_f)

    place = (lax.broadcasted_iota(jnp.int32, (PAIRS, B), 0) * 2 + c).astype(F32)
    sums = [jnp.zeros((PAIRS, B), F32), jnp.zeros((PAIRS, B), F32)]
    for cc in range(2):
        for xx in range(X):
            for l in range(MAXN):
                rows = got_x[cc * X + xx, l]
                child = place == rows[3:4]
                for q in range(2):
                    sums[q] = sums[q] + jnp.where(child, rows[q + 1 : q + 2], 0.0)
    for p in range(PAIRS):
        for q in range(2):
            acc[p, q : q + 1] = sums[q][p : p + 1]

    @pl.loop(0, PAIRS - 1)
    def _(n):
        to = chip_at(n)
        remote(acc.at[to], got_all.at[chip], send_g, recv_g, (to * 2 + c, x)).start()

    got_all[chip] = acc[chip]
    arrived(seven, send_f)
    for xx in range(X):
        for l in range(MAXN):
            def put(xx=xx, l=l):
                out[pl.ds(first(xx) + l, 1)] = got_x[c * X + xx, l, 0:1]

            if l < MAXN - 1:
                put()
            else:
                pl.when(count(xx) == MAXN)(put)
    arrived(got_all.at[0 : PAIRS - 1], recv_g)
    last = jnp.sum(got_all[...], 0)
    out[14:15] = last[0:1] - pfield[...].astype(F32) * last[1:2]
    arrived(got_all.at[0 : PAIRS - 1], send_g)


def split_rows(rows, leaf_grad, coupling_grad):
    leaf_grad[...] = rows[0:14]
    coupling_grad[...] = rows[14:15]


def body(parent_inverse, leaf_inverse, coupling, sensitivity, parent_of, leaf_field, parent_field):
    dma = pltpu.SemaphoreType.DMA
    hbm = pl.BlockSpec(memory_space=pltpu.HBM)
    vmem = pl.BlockSpec(memory_space=pltpu.VMEM)
    rows = pl.pallas_call(
        kernel,
        name="field_gradient",
        out_shape=jax.ShapeDtypeStruct((16, B), F32),
        in_specs=[pl.BlockSpec(memory_space=pltpu.SMEM), hbm, hbm, hbm, hbm, vmem, vmem],
        out_specs=vmem,
        scratch_shapes=[
            pltpu.VMEM((MAXN, W, W), BF16),
            pltpu.VMEM((MAXN, W, W), BF16),
            pltpu.VMEM((MAXN, W, W), BF16),
            pltpu.VMEM((MAXN, 2, 5, B, B), BF16),
            pltpu.VMEM((MAXN, W, W), F32),
            pltpu.VMEM((MAXN, W, W), BF16),
            pltpu.VMEM((MAXN, W, W), F32),
            pltpu.VMEM((W, W), BF16),
            pltpu.VMEM((W, W), BF16),
            pltpu.VMEM((GROUPS, YFIRST, B, B), BF16),
            pltpu.VMEM((GROUPS, 5 - YFIRST, B, B), BF16),
            pltpu.VMEM((2, MAXN, 5, B, B), BF16),
            pltpu.VMEM((14, B, W), BF16),
            pltpu.VMEM((14, B, W), BF16),
            pltpu.VMEM((14, B, W), BF16),
            pltpu.VMEM((16, W), F32),
            pltpu.VMEM((MAXN, 4, W), F32),
            pltpu.VMEM((2 * X, MAXN, 4, B), F32),
            pltpu.VMEM((PAIRS, 2, B), F32),
            pltpu.VMEM((PAIRS, 2, B), F32),
            dma((3,)),
            dma, dma, dma, dma, dma, dma((2,)), dma((2,)), dma, dma,
            dma, dma((MAXN,)), dma((MAXN,)), dma((MAXN,)), dma((14,)), dma((14,)), dma((2,)), dma, dma,
        ],
        compiler_params=pltpu.CompilerParams(
            collective_id=0, has_side_effects=True, vmem_limit_bytes=64 * 2**20
        ),
    )(parent_of.reshape(1, 14), parent_inverse, leaf_inverse, coupling, sensitivity, leaf_field, parent_field)
    return pl.pallas_call(
        split_rows,
        name="split_rows",
        out_shape=(jax.ShapeDtypeStruct((14, B), F32), jax.ShapeDtypeStruct((1, B), F32)),
        in_specs=[vmem],
        out_specs=(vmem, vmem),
    )(rows)


def solution(mesh):
    in_specs = (
        P("leaf", None, "blk"),
        P("leaf", "blk", None),
        P("leaf", "blk", None),
        P("leaf", "blk", None),
        P("leaf", None),
        P("leaf", None),
        P("leaf", "blk"),
    )
    out_specs = (P("leaf", "blk"), P("leaf", "blk"))
    return jax.shard_map(body, mesh=mesh, in_specs=in_specs, out_specs=out_specs, check_vma=False)
```

```python
import jax
import jax.numpy as jnp
from jax import lax
from jax.experimental import pallas as pl
from jax.experimental.pallas import tpu as pltpu
from jax.sharding import PartitionSpec as P

MESH = pl.DeviceIdType.MESH
F32 = jnp.float32
BF16 = jnp.bfloat16
B = 128
H = 64
W = 512
X, Y, Z = 4, 4, 8
GROUPS = 64
PAIRS = 32
MAXN = 4
EVEN = ((0, 0), (1, 0), (2, 0), (3, 0), (2, 2))
ODD = ((1, 1), (2, 1), (3, 1), (3, 3), (3, 2))
YFIRST = 2

BELOW = (1, 4, 5, 1)


def shares():
    table = {}
    for d, n in enumerate(BELOW):
        table[(d - 1) % X, 0] = (0, n) if n > 2 else (5 - n, 5)
        table[(d + 1) % X, 1] = (n, 5) if n > 2 else (0, 5 - n)
    return table


SHARES = shares()
EARLY = 2


def transposed_dot(a, b):
    return lax.dot_general(a, b, (((0,), (0,)), ((), ())), preferred_element_type=F32)


def at_block(i):
    return pl.ds(pl.multiple_of(i * B, B), B)


def kernel(
    pof, pinv, linv, coup, sens, field, pfield,
    out,
    cbuf, lbuf, sbuf, ublk, mixed, mixed_half, crossed, factor, cov, ga, gb, picked,
    vc, vl, vs, packed, halves, fld, fin, got_x, acc, got_all,
    load, send_d, recv_d,
    send_p, send_c, send_l, send_s, send_u, send_ring, send_cross, send_f, send_g,
    recv_p, recv_cl, recv_s, recv_u, recv_a, recv_b, recv_cross, recv_f, recv_g,
):
    leaf = lax.axis_index("leaf")
    x = lax.axis_index("blk")
    z = leaf // 8
    y = (leaf // 2) % 4
    c = leaf % 2

    def count(xx):
        return 3 + (xx + c + 1) % 2

    def first(xx):
        return 3 * xx + (xx + 1 - c) // 2

    def plane(d):
        return (x + d) % X

    def remote(src, dst, send, recv, to):
        return pltpu.make_async_remote_copy(src, dst, send, recv, device_id=to, device_id_type=MESH)

    mine = count(x)
    base = first(x)
    counts = [count(plane(d)) for d in range(X)]
    firsts = [first(plane(d)) for d in range(X)]

    def arrived(ref, sem):
        pltpu.make_async_copy(ref, ref, sem).wait()

    loads = [pltpu.make_async_copy(a, b, load.at[n]) for n, (a, b) in enumerate(((coup, vc), (linv, vl), (sens, vs)))]
    for copy in loads:
        copy.start()

    chip = leaf // 2
    other = leaf + 1 - 2 * c

    def chip_at(n):
        return (chip + (n + 15) % 31 + 1) % PAIRS

    barrier = pltpu.get_barrier_semaphore()

    def greet(*to):
        pl.semaphore_signal(barrier, inc=1, device_id=to, device_id_type=MESH)

    for d in (2, 1, 3):
        greet(leaf, plane(d))
    for d in (2, 1, 3, 0):
        greet(other, plane(d))
    for by in (1, -1):
        greet((z + by) % Z * 8 + y * 2 + c, x)
        greet(z * 8 + (y + by) % Y * 2 + c, x)

    zero = jnp.zeros((MAXN, B, B), BF16)
    lbuf[:, 0:B, B : 2 * B] = zero
    lbuf[:, 2 * B : 3 * B, 3 * B : 4 * B] = zero
    factor[0:B, B : 2 * B] = zero[0]
    factor[2 * B : 3 * B, 3 * B : 4 * B] = zero[0]
    fin[:, 0:3] = jnp.zeros((MAXN, 3, W), F32)
    fin[:, 3:4] = jnp.full((MAXN, 1, W), -1.0, F32)
    pl.semaphore_wait(barrier, 2 * X - 1 + 4)

    def slot_a(yy, zz, core=c):
        return core * 32 + zz * 4 + yy

    def slot_b(yy, zz, core=c):
        return core * 32 + yy * 8 + zz

    def own_slot(k):
        return ga.at[slot_a(y, z), k] if k < YFIRST else gb.at[slot_b(y, z), k - YFIRST]

    routes = [(0, k, k) for k in range(4)] + [(1, k, k + 1) for k in range(3)] + [(2, 4, 2), (3, 3, 3)]

    for at in range(X):
        @pl.when(x == at)
        def _(at=at):
            for plane_at, k, rb in routes:
                if plane_at == at:
                    block = pinv.at[0, rb * B : (rb + 1) * B]
                    remote(block, own_slot(k), send_p, recv_p, (leaf, plane(2))).start()
                    pltpu.make_async_copy(block, own_slot(k), recv_p).start()
            if at == 2:
                for d in (1, 3):
                    remote(pinv.at[0, 3 * B :], own_slot(4), send_p, recv_p, (leaf, plane(d))).start()

    def c_copy(d, l):
        return remote((vc if l else coup).at[firsts[d] + l], cbuf.at[l, at_block(x)], send_c, recv_cl.at[l], (leaf, plane(d)))

    def s_copy(d, l):
        return remote(vs.at[firsts[d] + l], sbuf.at[l, at_block(x)], send_s, recv_s.at[l], (leaf, plane(d)))

    def l_copy(d, l, cb):
        return remote((vl if l else linv).at[firsts[d] + l, :, at_block(cb)], lbuf.at[l, at_block(x), at_block(cb)],
                      send_l, recv_cl.at[l], (leaf, plane(d)))

    def l_half(d, l):
        return remote((vl if l else linv).at[firsts[d] + l, H:B, at_block(x)],
                      lbuf.at[l, pl.ds(pl.multiple_of(x * B + H, H), H), at_block(x)],
                      send_l, recv_cl.at[l], (leaf, plane(d)))

    low_lanes = lax.broadcasted_iota(jnp.int32, (H, B), 1) < H

    def quarters(d, pair):
        j = firsts[d] + 2 * pair
        one = vl[j, 0:H, at_block(x)].astype(F32)
        two = vl[jnp.minimum(j + 1, 13), 0:H, at_block(x)].astype(F32)
        return jnp.where(low_lanes, one, pltpu.roll(two, H, 1)).astype(BF16)

    def send_quarters():
        for pair in range(2):
            for d in (1, 3, 2):
                packed[d, pair] = quarters(d, pair)
                remote(packed.at[d, pair], halves.at[x, pair], send_d, recv_d, (leaf, plane(d))).start()
            halves[x, pair] = quarters(0, pair)

    def for_leaf(l, d, fn):
        if l < MAXN - 1:
            fn()
        else:
            pl.when(counts[d] == MAXN)(fn)

    def send_s_panels(leaves):
        for l in leaves:
            for d in (1, 3, 2):
                for_leaf(l, d, lambda l=l, d=d: s_copy(d, l).start())

    for l in range(MAXN):
        if l == 1:
            loads[0].wait()
            loads[1].wait()
            send_quarters()
        for d in (1, 3, 2):
            def send(l=l, d=d):
                c_copy(d, l).start()

                @pl.loop(0, x)
                def _(cb):
                    l_copy(d, l, cb).start()

                l_half(d, l).start()

            for_leaf(l, d, send)
    loads[2].wait()
    send_s_panels(range(EARLY))

    @pl.loop(0, mine)
    def _(l):
        pltpu.make_async_copy(vc.at[base + l], cbuf.at[l, at_block(x)], recv_cl.at[l]).start()
        pltpu.make_async_copy(vs.at[base + l], sbuf.at[l, at_block(x)], recv_s.at[l]).start()

        pltpu.make_async_copy(
            vl.at[base + l, H:B, at_block(x)],
            lbuf.at[l, pl.ds(pl.multiple_of(x * B + H, H), H), at_block(x)], recv_cl.at[l]).start()

        @pl.loop(0, x)
        def _(cb):
            pltpu.make_async_copy(
                vl.at[base + l, :, at_block(cb)], lbuf.at[l, at_block(x), at_block(cb)], recv_cl.at[l]).start()

    def up(n, v, by):
        return (v + by) % n

    def hop(which, ref, along_y, way, sem):
        by = 1 - 2 * way
        to = (z * 8 + up(Y, y, by) * 2 + c, x) if along_y else (up(Z, z, by) * 8 + y * 2 + c, x)
        remote(ref, ref, send_ring.at[which], sem, to).start()

    def a_first(step):
        for way in range(2):
            yy = up(Y, y, -(1 - 2 * way) * (step - 1))
            hop(0, ga.at[slot_a(yy, z)] if step == 1 else ga.at[slot_a(yy, z), way], True, way, recv_a.at[step - 1])

    def a_second(group, step):
        for way in range(2):
            zz = up(Z, z, -(1 - 2 * way) * (step - 1))
            sem = recv_a.at[2 + group * 4 + step - 1]
            if group == 1:
                for side in (way,) if step == 4 else range(2):
                    hop(0, ga.at[slot_a(up(Y, y, 2 * side - 1), zz)], False, way, sem)
            else:
                slot = slot_a(up(Y, y, group), zz)
                hop(0, ga.at[slot, way] if step == 4 else ga.at[slot], False, way, sem)

    def b_first(step):
        for way in range(2):
            slot = slot_b(y, up(Z, z, -(1 - 2 * way) * (step - 1)))
            ref = gb.at[slot, :, way * 64 : way * 64 + 64] if step == 4 else gb.at[slot]
            hop(1, ref, False, way, recv_b.at[step - 1])

    def b_second(group, step):
        for way in range(2):
            yy = up(Y, y, -(1 - 2 * way) * (step - 1))
            sem = recv_b.at[4 + group * 2 + step - 1]
            if group in (0, 4):
                slot = slot_b(yy, up(Z, z, group))
                hop(1, gb.at[slot, :, way * 64 : way * 64 + 64] if step == 2 else gb.at[slot], True, way, sem)
            else:
                for side in (way,) if step == 2 else range(2):
                    hop(1, gb.at[slot_b(yy, up(Z, z, (2 * side - 1) * group))], True, way, sem)

    def across_a(zz):
        ref = ga.at[pl.ds(slot_a(0, zz), 4)]
        remote(ref, ref, send_cross.at[0], recv_cross.at[0], (leaf + 1 - 2 * c, x)).start()

    def across_b(yy):
        ref = gb.at[pl.ds(slot_b(yy, 0), 8)]
        remote(ref, ref, send_cross.at[1], recv_cross.at[1], (leaf + 1 - 2 * c, x)).start()

    def a_first_done(step):
        arrived(ga.at[0 : 2 if step == 1 else 1], recv_a.at[step - 1])
        if step == 1:
            a_first(2)
            a_second(1, 1)
        else:
            a_second(2, 1)
            across_a(z)

    def a_second_done(group, step):
        size = (2 if step == 4 else 4) if group == 1 else (1 if step == 4 else 2)
        arrived(ga.at[0:size], recv_a.at[2 + group * 4 + step - 1])
        if step < 4:
            a_second(group, step + 1)

    def b_first_done(step):
        arrived(gb.at[0 : 1 if step == 4 else 2], recv_b.at[step - 1])
        if step < 4:
            b_first(step + 1)
        b_second(step, 1)
        if step == 4:
            across_b(y)

    def b_second_done(group, step):
        size = (1 if step == 2 else 2) if group in (0, 4) else (2 if step == 2 else 4)
        arrived(gb.at[0:size], recv_b.at[4 + group * 2 + step - 1])
        if step == 1:
            b_second(group, 2)

    arrived(picked.at[0, 0], recv_p)
    b_first(1)
    a_first(1)
    b_second(0, 1)
    a_second(0, 1)
    b_first_done(1)
    a_first_done(1)
    b_second_done(0, 1)
    a_second_done(0, 1)
    b_first_done(2)
    a_first_done(2)
    a_second_done(0, 2)
    b_second_done(1, 1)
    a_second_done(1, 1)
    b_first_done(3)
    a_second_done(2, 1)
    a_second_done(0, 3)
    b_second_done(2, 1)
    a_second_done(1, 2)
    b_first_done(4)
    a_second_done(2, 2)
    for way in range(2):
        across_a(up(Z, z, 2 * way - 1))
    b_second_done(3, 1)
    a_second_done(1, 3)
    a_second_done(2, 3)
    for step in range(2, 4):
        for way in range(2):
            across_a(up(Z, z, (2 * way - 1) * step))
    b_second_done(4, 1)
    for way in range(2):
        across_b(up(Y, y, 2 * way - 1))
    for group in range(3):
        a_second_done(group, 4)
    across_a(up(Z, z, 4))
    for group in range(5):
        b_second_done(group, 2)
    across_b(up(Y, y, 2))
    arrived(ga.at[0:32], recv_cross.at[0])
    arrived(gb.at[0:32], recv_cross.at[1])

    odd = x % 2

    def u_copy(i, l, low, high):
        return remote(picked.at[i, l, pl.ds(low, high - low)], ublk.at[l, odd, pl.ds(low, high - low)],
                      send_u, recv_u.at[l], (leaf, plane(1 + 2 * i)))

    def chosen(j):
        p = pof[0, j]
        half = (p & 1) * 32
        yy = (p >> 1) & 3
        zz = p >> 3
        a = half + zz * 4 + yy
        b = half + yy * 8 + zz
        return [lambda k=k: ga[a, k] for k in range(YFIRST)] + [lambda k=k: gb[b, k] for k in range(5 - YFIRST)]

    for l in range(MAXN):
        for i in range(2):
            def pick(l=l, i=i):
                block = chosen(firsts[1 + 2 * i] + l)

                for (at, way), (low, high) in SHARES.items():
                    if way == i and high > low:
                        @pl.when(x == at)
                        def _(low=low, high=high):
                            for k in range(low, high):
                                picked[i, l, k] = block[k]()
                            u_copy(i, l, low, high).start()

            for_leaf(l, 1 + 2 * i, pick)
    send_s_panels(range(EARLY, MAXN))

    for l in range(MAXN):
        def keep(l=l):
            block = chosen(base + l)
            for k in range(5):
                ublk[l, odd, k] = block[k]()

        for_leaf(l, 0, keep)

    fld[0:14] = field[...].astype(F32)

    @pl.loop(0, mine)
    def _(l):
        fin[l, 3:4] = jnp.full((1, W), pof[0, base + l].astype(F32))

    for at, blocks in enumerate((4, 3, 3, 1)):
        @pl.when(x == at)
        def _(blocks=blocks):
            arrived(pinv.at[0, 0 : blocks * B], send_p)
    arrived(ga.at[0:31], send_ring.at[0])
    arrived(gb.at[0:31], send_ring.at[1])
    arrived(ga.at[0:32], send_cross.at[0])
    arrived(gb.at[0:32], send_cross.at[1])

    arrived(halves.at[0 : X - 1], recv_d)
    for l in range(MAXN):
        for rb in range(X):
            quarter = halves[rb, l // 2].astype(F32)
            if l % 2:
                quarter = pltpu.roll(quarter, H, 1)
            lbuf[l, rb * B : rb * B + H, rb * B : (rb + 1) * B] = jnp.where(low_lanes, quarter, 0.0).astype(BF16)

    @pl.loop(0, mine)
    def _(l):
        arrived(ga.at[0:12], recv_cl.at[l])

        left = jnp.dot(cbuf[l], lbuf[l, :, 0 : 2 * B], preferred_element_type=F32)
        mixed[l, :, 0 : 2 * B] = left
        mixed_half[l, :, 0 : 2 * B] = left.astype(BF16)
        right = jnp.dot(cbuf[l, :, 2 * B :], lbuf[l, 2 * B :, 2 * B :], preferred_element_type=F32)
        mixed[l, :, 2 * B :] = right
        mixed_half[l, :, 2 * B :] = right.astype(BF16)
        low = lbuf[l, :, 0 : 2 * B].astype(F32)
        high = lbuf[l, 2 * B :, 2 * B :].astype(F32)
        fin[l, 0:1, 0 : 2 * B] = jnp.sum(low * low, 0, keepdims=True)
        fin[l, 0:1, 2 * B :] = jnp.sum(high * high, 0, keepdims=True)

    @pl.loop(0, mine)
    def _(l):
        arrived(ublk.at[l, 1 - odd], recv_u.at[l])
        for whose, blocks in enumerate((EVEN, ODD)):
            for k, (rb, cb) in enumerate(blocks):
                factor[rb * B : (rb + 1) * B, cb * B : (cb + 1) * B] = ublk[l, whose, k]
        u1 = factor[:, 0 : 2 * B]
        u21 = factor[2 * B :, 0 : 2 * B]
        u2 = factor[2 * B :, 2 * B :]
        cov[0 : 2 * B, 0 : 2 * B] = transposed_dot(u1, u1).astype(BF16)
        cov[0 : 2 * B, 2 * B :] = transposed_dot(u21, u2).astype(BF16)
        cov[2 * B :, 0 : 2 * B] = transposed_dot(u2, u21).astype(BF16)
        cov[2 * B :, 2 * B :] = transposed_dot(u2, u2).astype(BF16)
        total = jnp.zeros((1, W), F32)
        for rb in range(4):
            rows = slice(rb * B, (rb + 1) * B)
            cross = -jnp.dot(cov[rows], mixed_half[l], preferred_element_type=F32)
            crossed[l, rows] = cross
            half = cross.astype(BF16).astype(F32)
            total = total + jnp.sum(half * mixed[l, rows], 0, keepdims=True)
        value = fld[pl.ds(base + l, 1)]
        fin[l, 0:1] = 0.5 * (fin[l, 0:1] - total - value * value)

    arrived(packed.at[1:X], send_d)
    for most in range(2):
        @pl.when(mine == 3 + most)
        def _(most=most):
            arrived(vc.at[0 : 11 - most], send_c)
            for at in range(X):
                @pl.when(x == at)
                def _(at=at):
                    arrived(vl.at[0 : 11 - most, 0:H, 0:B], send_l)
                    if at:
                        arrived(vl.at[0 : 11 - most, :, 0 : at * B], send_l)

    @pl.loop(0, mine)
    def _(l):
        arrived(sbuf.at[l], recv_s.at[l])
        value = fld[pl.ds(base + l, 1)].astype(BF16)
        fin[l, 2:3] = lax.dot_general(value, sbuf[l], (((1,), (1,)), ((), ())), preferred_element_type=F32)
        for rb in range(4):
            rows = slice(rb * B, (rb + 1) * B)
            prod = sbuf[l, rows].astype(F32) * crossed[l, rows]
            prod = prod[:, 0:B] + prod[:, B : 2 * B] + prod[:, 2 * B : 3 * B] + prod[:, 3 * B :]
            fin[l, 1:2, rows] = jnp.sum(prod.T, 0, keepdims=True)

    for d in (2, 1, 3, 0):
        for to in (other, leaf) if d else (other,):
            remote(fin.at[:, :, at_block(plane(d))], got_x.at[c * X + x], send_f, recv_f, (to, plane(d))).start()
    got_x[c * X + x] = fin[:, :, at_block(x)]
    for most in range(2):
        @pl.when(mine == 3 + most)
        def _(most=most):
            arrived(vs.at[0 : 11 - most], send_s)

            for (at, way), (low, high) in SHARES.items():
                if high > low:
                    @pl.when(x == at)
                    def _(way=way, low=low, high=high):
                        arrived(picked.at[way, 0 : 4 - most, low:high], send_u)
    seven = got_x.at[0 : 2 * X - 1]
    arrived(seven, recv_f)

    place = (lax.broadcasted_iota(jnp.int32, (PAIRS, B), 0) * 2 + c).astype(F32)
    sums = [jnp.zeros((PAIRS, B), F32), jnp.zeros((PAIRS, B), F32)]
    for cc in range(2):
        for xx in range(X):
            for l in range(MAXN):
                rows = got_x[cc * X + xx, l]
                child = place == rows[3:4]
                for q in range(2):
                    sums[q] = sums[q] + jnp.where(child, rows[q + 1 : q + 2], 0.0)
    for p in range(PAIRS):
        for q in range(2):
            acc[p, q : q + 1] = sums[q][p : p + 1]

    @pl.loop(0, PAIRS - 1)
    def _(n):
        to = chip_at(n)
        remote(acc.at[to], got_all.at[chip], send_g, recv_g, (to * 2 + c, x)).start()

    got_all[chip] = acc[chip]
    arrived(seven, send_f)
    for xx in range(X):
        for l in range(MAXN):
            def put(xx=xx, l=l):
                out[pl.ds(first(xx) + l, 1)] = got_x[c * X + xx, l, 0:1]

            if l < MAXN - 1:
                put()
            else:
                pl.when(count(xx) == MAXN)(put)
    arrived(got_all.at[0 : PAIRS - 1], recv_g)
    last = jnp.sum(got_all[...], 0)
    out[14:15] = last[0:1] - pfield[...].astype(F32) * last[1:2]
    arrived(got_all.at[0 : PAIRS - 1], send_g)


def split_rows(rows, leaf_grad, coupling_grad):
    leaf_grad[...] = rows[0:14]
    coupling_grad[...] = rows[14:15]


def body(parent_inverse, leaf_inverse, coupling, sensitivity, parent_of, leaf_field, parent_field):
    dma = pltpu.SemaphoreType.DMA
    hbm = pl.BlockSpec(memory_space=pltpu.HBM)
    vmem = pl.BlockSpec(memory_space=pltpu.VMEM)
    rows = pl.pallas_call(
        kernel,
        name="field_gradient",
        out_shape=jax.ShapeDtypeStruct((16, B), F32),
        in_specs=[pl.BlockSpec(memory_space=pltpu.SMEM), hbm, hbm, hbm, hbm, vmem, vmem],
        out_specs=vmem,
        scratch_shapes=[
            pltpu.VMEM((MAXN, W, W), BF16),
            pltpu.VMEM((MAXN, W, W), BF16),
            pltpu.VMEM((MAXN, W, W), BF16),
            pltpu.VMEM((MAXN, 2, 5, B, B), BF16),
            pltpu.VMEM((MAXN, W, W), F32),
            pltpu.VMEM((MAXN, W, W), BF16),
            pltpu.VMEM((MAXN, W, W), F32),
            pltpu.VMEM((W, W), BF16),
            pltpu.VMEM((W, W), BF16),
            pltpu.VMEM((GROUPS, YFIRST, B, B), BF16),
            pltpu.VMEM((GROUPS, 5 - YFIRST, B, B), BF16),
            pltpu.VMEM((2, MAXN, 5, B, B), BF16),
            pltpu.VMEM((14, B, W), BF16),
            pltpu.VMEM((14, B, W), BF16),
            pltpu.VMEM((14, B, W), BF16),
            pltpu.VMEM((X, 2, H, B), BF16),
            pltpu.VMEM((X, 2, H, B), BF16),
            pltpu.VMEM((16, W), F32),
            pltpu.VMEM((MAXN, 4, W), F32),
            pltpu.VMEM((2 * X, MAXN, 4, B), F32),
            pltpu.VMEM((PAIRS, 2, B), F32),
            pltpu.VMEM((PAIRS, 2, B), F32),
            dma((3,)), dma, dma,
            dma, dma, dma, dma, dma, dma((2,)), dma((2,)), dma, dma,
            dma, dma((MAXN,)), dma((MAXN,)), dma((MAXN,)), dma((14,)), dma((14,)), dma((2,)), dma, dma,
        ],
        compiler_params=pltpu.CompilerParams(
            collective_id=0, has_side_effects=True, vmem_limit_bytes=64 * 2**20
        ),
    )(parent_of.reshape(1, 14), parent_inverse, leaf_inverse, coupling, sensitivity, leaf_field, parent_field)
    return pl.pallas_call(
        split_rows,
        name="split_rows",
        out_shape=(jax.ShapeDtypeStruct((14, B), F32), jax.ShapeDtypeStruct((1, B), F32)),
        in_specs=[vmem],
        out_specs=(vmem, vmem),
    )(rows)


def solution(mesh):
    in_specs = (
        P("leaf", None, "blk"),
        P("leaf", "blk", None),
        P("leaf", "blk", None),
        P("leaf", "blk", None),
        P("leaf", None),
        P("leaf", None),
        P("leaf", "blk"),
    )
    out_specs = (P("leaf", "blk"), P("leaf", "blk"))
    return jax.shard_map(body, mesh=mesh, in_specs=in_specs, out_specs=out_specs, check_vma=False)
```

```python
import jax
import jax.numpy as jnp
from jax import lax
from jax.experimental import pallas as pl
from jax.experimental.pallas import tpu as pltpu
from jax.sharding import PartitionSpec as P

MESH = pl.DeviceIdType.MESH
F32 = jnp.float32
BF16 = jnp.bfloat16
B = 128
H = 64
W = 512
X, Y, Z = 4, 4, 8
GROUPS = 64
PAIRS = 32
MAXN = 4
EVEN = ((0, 0), (1, 0), (2, 0), (3, 0), (2, 2))
ODD = ((1, 1), (2, 1), (3, 1), (3, 3), (3, 2))
YFIRST = 2

BELOW = (1, 4, 5, 1)


def shares():
    table = {}
    for d, n in enumerate(BELOW):
        table[(d - 1) % X, 0] = (0, n) if n > 2 else (5 - n, 5)
        table[(d + 1) % X, 1] = (n, 5) if n > 2 else (0, 5 - n)
    return table


SHARES = shares()
EARLY = 2


def transposed_dot(a, b):
    return lax.dot_general(a, b, (((0,), (0,)), ((), ())), preferred_element_type=F32)


def at_block(i):
    return pl.ds(pl.multiple_of(i * B, B), B)


def kernel(
    parents, pinv, linv, coup, sens, fields, pfields,
    out,
    cbuf, lbuf, sbuf, ublk, mixed, mixed_half, crossed, factor, cov, ga, gb, picked,
    vc, vl, vs, packed, halves, fld, fin, got_x, acc, got_all,
    pof, field, pfield, load, send_d, recv_d,
    send_p, send_c, send_l, send_s, send_u, send_ring, send_cross, send_f, send_g,
    recv_p, recv_cl, recv_s, recv_u, recv_a, recv_b, recv_cross, recv_f, recv_g,
):
    leaf = lax.axis_index("leaf")
    x = lax.axis_index("blk")
    z = leaf // 8
    y = (leaf // 2) % 4
    c = leaf % 2

    def count(xx):
        return 3 + (xx + c + 1) % 2

    def first(xx):
        return 3 * xx + (xx + 1 - c) // 2

    def plane(d):
        return (x + d) % X

    def remote(src, dst, send, recv, to):
        return pltpu.make_async_remote_copy(src, dst, send, recv, device_id=to, device_id_type=MESH)

    mine = count(x)
    base = first(x)
    counts = [count(plane(d)) for d in range(X)]
    firsts = [first(plane(d)) for d in range(X)]

    def arrived(ref, sem):
        pltpu.make_async_copy(ref, ref, sem).wait()

    loads = [pltpu.make_async_copy(a, b, load.at[n]) for n, (a, b) in enumerate(((coup, vc), (linv, vl), (sens, vs), (parents, pof), (fields, field), (pfields, pfield)))]
    for copy in loads:
        copy.start()

    chip = leaf // 2
    other = leaf + 1 - 2 * c

    def chip_at(n):
        return (chip + (n + 15) % 31 + 1) % PAIRS

    barrier = pltpu.get_barrier_semaphore()

    def greet(*to):
        pl.semaphore_signal(barrier, inc=1, device_id=to, device_id_type=MESH)

    for d in (2, 1, 3):
        greet(leaf, plane(d))
    for d in (2, 1, 3, 0):
        greet(other, plane(d))
    for by in (1, -1):
        greet((z + by) % Z * 8 + y * 2 + c, x)
        greet(z * 8 + (y + by) % Y * 2 + c, x)

    zero = jnp.zeros((MAXN, B, B), BF16)
    lbuf[:, 0:B, B : 2 * B] = zero
    lbuf[:, 2 * B : 3 * B, 3 * B : 4 * B] = zero
    factor[0:B, B : 2 * B] = zero[0]
    factor[2 * B : 3 * B, 3 * B : 4 * B] = zero[0]
    fin[:, 0:3] = jnp.zeros((MAXN, 3, W), F32)
    fin[:, 3:4] = jnp.full((MAXN, 1, W), -1.0, F32)
    pl.semaphore_wait(barrier, 2 * X - 1 + 4)

    def slot_a(yy, zz, core=c):
        return core * 32 + zz * 4 + yy

    def slot_b(yy, zz, core=c):
        return core * 32 + yy * 8 + zz

    def own_slot(k):
        return ga.at[slot_a(y, z), k] if k < YFIRST else gb.at[slot_b(y, z), k - YFIRST]

    routes = [(0, k, k) for k in range(4)] + [(1, k, k + 1) for k in range(3)] + [(2, 4, 2), (3, 3, 3)]

    for at in range(X):
        @pl.when(x == at)
        def _(at=at):
            for plane_at, k, rb in routes:
                if plane_at == at:
                    block = pinv.at[0, rb * B : (rb + 1) * B]
                    remote(block, own_slot(k), send_p, recv_p, (leaf, plane(2))).start()
                    pltpu.make_async_copy(block, own_slot(k), recv_p).start()
            if at == 2:
                for d in (1, 3):
                    remote(pinv.at[0, 3 * B :], own_slot(4), send_p, recv_p, (leaf, plane(d))).start()

    def c_copy(d, l):
        return remote((vc if l else coup).at[firsts[d] + l], cbuf.at[l, at_block(x)], send_c, recv_cl.at[l], (leaf, plane(d)))

    def s_copy(d, l):
        return remote(vs.at[firsts[d] + l], sbuf.at[l, at_block(x)], send_s, recv_s.at[l], (leaf, plane(d)))

    def l_copy(d, l, cb):
        return remote((vl if l else linv).at[firsts[d] + l, :, at_block(cb)], lbuf.at[l, at_block(x), at_block(cb)],
                      send_l, recv_cl.at[l], (leaf, plane(d)))

    def l_half(d, l):
        return remote((vl if l else linv).at[firsts[d] + l, H:B, at_block(x)],
                      lbuf.at[l, pl.ds(pl.multiple_of(x * B + H, H), H), at_block(x)],
                      send_l, recv_cl.at[l], (leaf, plane(d)))

    low_lanes = lax.broadcasted_iota(jnp.int32, (H, B), 1) < H

    def quarters(d, pair):
        j = firsts[d] + 2 * pair
        one = vl[j, 0:H, at_block(x)].astype(F32)
        two = vl[jnp.minimum(j + 1, 13), 0:H, at_block(x)].astype(F32)
        return jnp.where(low_lanes, one, pltpu.roll(two, H, 1)).astype(BF16)

    def send_quarters():
        for pair in range(2):
            for d in (1, 3, 2):
                packed[d, pair] = quarters(d, pair)
                remote(packed.at[d, pair], halves.at[x, pair], send_d, recv_d, (leaf, plane(d))).start()
            halves[x, pair] = quarters(0, pair)

    def for_leaf(l, d, fn):
        if l < MAXN - 1:
            fn()
        else:
            pl.when(counts[d] == MAXN)(fn)

    def send_s_panels(leaves):
        for l in leaves:
            for d in (1, 3, 2):
                for_leaf(l, d, lambda l=l, d=d: s_copy(d, l).start())

    for l in range(MAXN):
        if l == 1:
            loads[0].wait()
            loads[1].wait()
            send_quarters()
        for d in (1, 3, 2):
            def send(l=l, d=d):
                c_copy(d, l).start()

                @pl.loop(0, x)
                def _(cb):
                    l_copy(d, l, cb).start()

                l_half(d, l).start()

            for_leaf(l, d, send)
    loads[2].wait()
    send_s_panels(range(EARLY))

    @pl.loop(0, mine)
    def _(l):
        pltpu.make_async_copy(vc.at[base + l], cbuf.at[l, at_block(x)], recv_cl.at[l]).start()
        pltpu.make_async_copy(vs.at[base + l], sbuf.at[l, at_block(x)], recv_s.at[l]).start()

        pltpu.make_async_copy(
            vl.at[base + l, H:B, at_block(x)],
            lbuf.at[l, pl.ds(pl.multiple_of(x * B + H, H), H), at_block(x)], recv_cl.at[l]).start()

        @pl.loop(0, x)
        def _(cb):
            pltpu.make_async_copy(
                vl.at[base + l, :, at_block(cb)], lbuf.at[l, at_block(x), at_block(cb)], recv_cl.at[l]).start()

    def up(n, v, by):
        return (v + by) % n

    def hop(which, ref, along_y, way, sem):
        by = 1 - 2 * way
        to = (z * 8 + up(Y, y, by) * 2 + c, x) if along_y else (up(Z, z, by) * 8 + y * 2 + c, x)
        remote(ref, ref, send_ring.at[which], sem, to).start()

    def a_first(step):
        for way in range(2):
            yy = up(Y, y, -(1 - 2 * way) * (step - 1))
            hop(0, ga.at[slot_a(yy, z)] if step == 1 else ga.at[slot_a(yy, z), way], True, way, recv_a.at[step - 1])

    def a_second(group, step):
        for way in range(2):
            zz = up(Z, z, -(1 - 2 * way) * (step - 1))
            sem = recv_a.at[2 + group * 4 + step - 1]
            if group == 1:
                for side in (way,) if step == 4 else range(2):
                    hop(0, ga.at[slot_a(up(Y, y, 2 * side - 1), zz)], False, way, sem)
            else:
                slot = slot_a(up(Y, y, group), zz)
                hop(0, ga.at[slot, way] if step == 4 else ga.at[slot], False, way, sem)

    def b_first(step):
        for way in range(2):
            slot = slot_b(y, up(Z, z, -(1 - 2 * way) * (step - 1)))
            ref = gb.at[slot, :, way * 64 : way * 64 + 64] if step == 4 else gb.at[slot]
            hop(1, ref, False, way, recv_b.at[step - 1])

    def b_second(group, step):
        for way in range(2):
            yy = up(Y, y, -(1 - 2 * way) * (step - 1))
            sem = recv_b.at[4 + group * 2 + step - 1]
            if group in (0, 4):
                slot = slot_b(yy, up(Z, z, group))
                hop(1, gb.at[slot, :, way * 64 : way * 64 + 64] if step == 2 else gb.at[slot], True, way, sem)
            else:
                for side in (way,) if step == 2 else range(2):
                    hop(1, gb.at[slot_b(yy, up(Z, z, (2 * side - 1) * group))], True, way, sem)

    def across_a(zz):
        ref = ga.at[pl.ds(slot_a(0, zz), 4)]
        remote(ref, ref, send_cross.at[0], recv_cross.at[0], (leaf + 1 - 2 * c, x)).start()

    def across_b(yy):
        ref = gb.at[pl.ds(slot_b(yy, 0), 8)]
        remote(ref, ref, send_cross.at[1], recv_cross.at[1], (leaf + 1 - 2 * c, x)).start()

    def a_first_done(step):
        arrived(ga.at[0 : 2 if step == 1 else 1], recv_a.at[step - 1])
        if step == 1:
            a_first(2)
            a_second(1, 1)
        else:
            a_second(2, 1)
            across_a(z)

    def a_second_done(group, step):
        size = (2 if step == 4 else 4) if group == 1 else (1 if step == 4 else 2)
        arrived(ga.at[0:size], recv_a.at[2 + group * 4 + step - 1])
        if step < 4:
            a_second(group, step + 1)

    def b_first_done(step):
        arrived(gb.at[0 : 1 if step == 4 else 2], recv_b.at[step - 1])
        if step < 4:
            b_first(step + 1)
        b_second(step, 1)
        if step == 4:
            across_b(y)

    def b_second_done(group, step):
        size = (1 if step == 2 else 2) if group in (0, 4) else (2 if step == 2 else 4)
        arrived(gb.at[0:size], recv_b.at[4 + group * 2 + step - 1])
        if step == 1:
            b_second(group, 2)

    arrived(picked.at[0, 0], recv_p)
    b_first(1)
    a_first(1)
    b_second(0, 1)
    a_second(0, 1)
    b_first_done(1)
    a_first_done(1)
    b_second_done(0, 1)
    a_second_done(0, 1)
    b_first_done(2)
    a_first_done(2)
    a_second_done(0, 2)
    b_second_done(1, 1)
    a_second_done(1, 1)
    b_first_done(3)
    a_second_done(2, 1)
    a_second_done(0, 3)
    b_second_done(2, 1)
    a_second_done(1, 2)
    b_first_done(4)
    a_second_done(2, 2)
    for way in range(2):
        across_a(up(Z, z, 2 * way - 1))
    b_second_done(3, 1)
    a_second_done(1, 3)
    a_second_done(2, 3)
    for step in range(2, 4):
        for way in range(2):
            across_a(up(Z, z, (2 * way - 1) * step))
    b_second_done(4, 1)
    for way in range(2):
        across_b(up(Y, y, 2 * way - 1))
    for group in range(3):
        a_second_done(group, 4)
    across_a(up(Z, z, 4))
    for group in range(5):
        b_second_done(group, 2)
    across_b(up(Y, y, 2))
    arrived(ga.at[0:32], recv_cross.at[0])
    arrived(gb.at[0:32], recv_cross.at[1])

    odd = x % 2

    def u_copy(i, l, low, high):
        return remote(picked.at[i, l, pl.ds(low, high - low)], ublk.at[l, odd, pl.ds(low, high - low)],
                      send_u, recv_u.at[l], (leaf, plane(1 + 2 * i)))

    def chosen(j):
        p = pof[0, j]
        half = (p & 1) * 32
        yy = (p >> 1) & 3
        zz = p >> 3
        a = half + zz * 4 + yy
        b = half + yy * 8 + zz
        return [lambda k=k: ga[a, k] for k in range(YFIRST)] + [lambda k=k: gb[b, k] for k in range(5 - YFIRST)]

    loads[3].wait()
    for l in range(MAXN):
        for i in range(2):
            def pick(l=l, i=i):
                block = chosen(firsts[1 + 2 * i] + l)

                for (at, way), (low, high) in SHARES.items():
                    if way == i and high > low:
                        @pl.when(x == at)
                        def _(low=low, high=high):
                            for k in range(low, high):
                                picked[i, l, k] = block[k]()
                            u_copy(i, l, low, high).start()

            for_leaf(l, 1 + 2 * i, pick)
    send_s_panels(range(EARLY, MAXN))

    for l in range(MAXN):
        def keep(l=l):
            block = chosen(base + l)
            for k in range(5):
                ublk[l, odd, k] = block[k]()

        for_leaf(l, 0, keep)

    loads[4].wait()
    loads[5].wait()
    fld[0:14] = field[...].astype(F32)

    @pl.loop(0, mine)
    def _(l):
        fin[l, 3:4] = jnp.full((1, W), pof[0, base + l].astype(F32))

    for at, blocks in enumerate((4, 3, 3, 1)):
        @pl.when(x == at)
        def _(blocks=blocks):
            arrived(pinv.at[0, 0 : blocks * B], send_p)
    arrived(ga.at[0:31], send_ring.at[0])
    arrived(gb.at[0:31], send_ring.at[1])
    arrived(ga.at[0:32], send_cross.at[0])
    arrived(gb.at[0:32], send_cross.at[1])

    arrived(halves.at[0 : X - 1], recv_d)
    for l in range(MAXN):
        for rb in range(X):
            quarter = halves[rb, l // 2].astype(F32)
            if l % 2:
                quarter = pltpu.roll(quarter, H, 1)
            lbuf[l, rb * B : rb * B + H, rb * B : (rb + 1) * B] = jnp.where(low_lanes, quarter, 0.0).astype(BF16)

    @pl.loop(0, mine)
    def _(l):
        arrived(ga.at[0:12], recv_cl.at[l])

        left = jnp.dot(cbuf[l], lbuf[l, :, 0 : 2 * B], preferred_element_type=F32)
        mixed[l, :, 0 : 2 * B] = left
        mixed_half[l, :, 0 : 2 * B] = left.astype(BF16)
        right = jnp.dot(cbuf[l, :, 2 * B :], lbuf[l, 2 * B :, 2 * B :], preferred_element_type=F32)
        mixed[l, :, 2 * B :] = right
        mixed_half[l, :, 2 * B :] = right.astype(BF16)
        low = lbuf[l, :, 0 : 2 * B].astype(F32)
        high = lbuf[l, 2 * B :, 2 * B :].astype(F32)
        fin[l, 0:1, 0 : 2 * B] = jnp.sum(low * low, 0, keepdims=True)
        fin[l, 0:1, 2 * B :] = jnp.sum(high * high, 0, keepdims=True)

    @pl.loop(0, mine)
    def _(l):
        arrived(ublk.at[l, 1 - odd], recv_u.at[l])
        for whose, blocks in enumerate((EVEN, ODD)):
            for k, (rb, cb) in enumerate(blocks):
                factor[rb * B : (rb + 1) * B, cb * B : (cb + 1) * B] = ublk[l, whose, k]
        u1 = factor[:, 0 : 2 * B]
        u21 = factor[2 * B :, 0 : 2 * B]
        u2 = factor[2 * B :, 2 * B :]
        cov[0 : 2 * B, 0 : 2 * B] = transposed_dot(u1, u1).astype(BF16)
        cov[0 : 2 * B, 2 * B :] = transposed_dot(u21, u2).astype(BF16)
        cov[2 * B :, 0 : 2 * B] = transposed_dot(u2, u21).astype(BF16)
        cov[2 * B :, 2 * B :] = transposed_dot(u2, u2).astype(BF16)
        total = jnp.zeros((1, W), F32)
        for rb in range(4):
            rows = slice(rb * B, (rb + 1) * B)
            cross = -jnp.dot(cov[rows], mixed_half[l], preferred_element_type=F32)
            crossed[l, rows] = cross
            half = cross.astype(BF16).astype(F32)
            total = total + jnp.sum(half * mixed[l, rows], 0, keepdims=True)
        value = fld[pl.ds(base + l, 1)]
        fin[l, 0:1] = 0.5 * (fin[l, 0:1] - total - value * value)

    arrived(packed.at[1:X], send_d)
    for most in range(2):
        @pl.when(mine == 3 + most)
        def _(most=most):
            arrived(vc.at[0 : 11 - most], send_c)
            for at in range(X):
                @pl.when(x == at)
                def _(at=at):
                    arrived(vl.at[0 : 11 - most, 0:H, 0:B], send_l)
                    if at:
                        arrived(vl.at[0 : 11 - most, :, 0 : at * B], send_l)

    @pl.loop(0, mine)
    def _(l):
        arrived(sbuf.at[l], recv_s.at[l])
        value = fld[pl.ds(base + l, 1)].astype(BF16)
        fin[l, 2:3] = lax.dot_general(value, sbuf[l], (((1,), (1,)), ((), ())), preferred_element_type=F32)
        for rb in range(4):
            rows = slice(rb * B, (rb + 1) * B)
            prod = sbuf[l, rows].astype(F32) * crossed[l, rows]
            prod = prod[:, 0:B] + prod[:, B : 2 * B] + prod[:, 2 * B : 3 * B] + prod[:, 3 * B :]
            fin[l, 1:2, rows] = jnp.sum(prod.T, 0, keepdims=True)

    for d in (2, 1, 3, 0):
        for to in (other, leaf) if d else (other,):
            remote(fin.at[:, :, at_block(plane(d))], got_x.at[c * X + x], send_f, recv_f, (to, plane(d))).start()
    got_x[c * X + x] = fin[:, :, at_block(x)]
    for most in range(2):
        @pl.when(mine == 3 + most)
        def _(most=most):
            arrived(vs.at[0 : 11 - most], send_s)

            for (at, way), (low, high) in SHARES.items():
                if high > low:
                    @pl.when(x == at)
                    def _(way=way, low=low, high=high):
                        arrived(picked.at[way, 0 : 4 - most, low:high], send_u)
    seven = got_x.at[0 : 2 * X - 1]
    arrived(seven, recv_f)

    place = (lax.broadcasted_iota(jnp.int32, (PAIRS, B), 0) * 2 + c).astype(F32)
    sums = [jnp.zeros((PAIRS, B), F32), jnp.zeros((PAIRS, B), F32)]
    for cc in range(2):
        for xx in range(X):
            for l in range(MAXN):
                rows = got_x[cc * X + xx, l]
                child = place == rows[3:4]
                for q in range(2):
                    sums[q] = sums[q] + jnp.where(child, rows[q + 1 : q + 2], 0.0)
    for p in range(PAIRS):
        for q in range(2):
            acc[p, q : q + 1] = sums[q][p : p + 1]

    @pl.loop(0, PAIRS - 1)
    def _(n):
        to = chip_at(n)
        remote(acc.at[to], got_all.at[chip], send_g, recv_g, (to * 2 + c, x)).start()

    got_all[chip] = acc[chip]
    arrived(seven, send_f)
    for xx in range(X):
        for l in range(MAXN):
            def put(xx=xx, l=l):
                out[pl.ds(first(xx) + l, 1)] = got_x[c * X + xx, l, 0:1]

            if l < MAXN - 1:
                put()
            else:
                pl.when(count(xx) == MAXN)(put)
    arrived(got_all.at[0 : PAIRS - 1], recv_g)
    last = jnp.sum(got_all[...], 0)
    out[14:15] = last[0:1] - pfield[...].astype(F32) * last[1:2]
    arrived(got_all.at[0 : PAIRS - 1], send_g)


def split_rows(rows, leaf_grad, coupling_grad):
    leaf_grad[...] = rows[0:14]
    coupling_grad[...] = rows[14:15]


def body(parent_inverse, leaf_inverse, coupling, sensitivity, parent_of, leaf_field, parent_field):
    dma = pltpu.SemaphoreType.DMA
    hbm = pl.BlockSpec(memory_space=pltpu.HBM)
    vmem = pl.BlockSpec(memory_space=pltpu.VMEM)
    rows = pl.pallas_call(
        kernel,
        name="field_gradient",
        out_shape=jax.ShapeDtypeStruct((16, B), F32),
        in_specs=[hbm] * 7,
        out_specs=vmem,
        scratch_shapes=[
            pltpu.VMEM((MAXN, W, W), BF16),
            pltpu.VMEM((MAXN, W, W), BF16),
            pltpu.VMEM((MAXN, W, W), BF16),
            pltpu.VMEM((MAXN, 2, 5, B, B), BF16),
            pltpu.VMEM((MAXN, W, W), F32),
            pltpu.VMEM((MAXN, W, W), BF16),
            pltpu.VMEM((MAXN, W, W), F32),
            pltpu.VMEM((W, W), BF16),
            pltpu.VMEM((W, W), BF16),
            pltpu.VMEM((GROUPS, YFIRST, B, B), BF16),
            pltpu.VMEM((GROUPS, 5 - YFIRST, B, B), BF16),
            pltpu.VMEM((2, MAXN, 5, B, B), BF16),
            pltpu.VMEM((14, B, W), BF16),
            pltpu.VMEM((14, B, W), BF16),
            pltpu.VMEM((14, B, W), BF16),
            pltpu.VMEM((X, 2, H, B), BF16),
            pltpu.VMEM((X, 2, H, B), BF16),
            pltpu.VMEM((16, W), F32),
            pltpu.VMEM((MAXN, 4, W), F32),
            pltpu.VMEM((2 * X, MAXN, 4, B), F32),
            pltpu.VMEM((PAIRS, 2, B), F32),
            pltpu.VMEM((PAIRS, 2, B), F32),
            pltpu.SMEM((1, 14), jnp.int32),
            pltpu.VMEM((14, W), BF16),
            pltpu.VMEM((1, B), BF16),
            dma((6,)), dma, dma,
            dma, dma, dma, dma, dma, dma((2,)), dma((2,)), dma, dma,
            dma, dma((MAXN,)), dma((MAXN,)), dma((MAXN,)), dma((14,)), dma((14,)), dma((2,)), dma, dma,
        ],
        compiler_params=pltpu.CompilerParams(
            collective_id=0, has_side_effects=True, vmem_limit_bytes=64 * 2**20
        ),
    )(parent_of.reshape(1, 14), parent_inverse, leaf_inverse, coupling, sensitivity, leaf_field, parent_field)
    return pl.pallas_call(
        split_rows,
        name="split_rows",
        out_shape=(jax.ShapeDtypeStruct((14, B), F32), jax.ShapeDtypeStruct((1, B), F32)),
        in_specs=[vmem],
        out_specs=(vmem, vmem),
    )(rows)


def solution(mesh):
    in_specs = (
        P("leaf", None, "blk"),
        P("leaf", "blk", None),
        P("leaf", "blk", None),
        P("leaf", "blk", None),
        P("leaf", None),
        P("leaf", None),
        P("leaf", "blk"),
    )
    out_specs = (P("leaf", "blk"), P("leaf", "blk"))
    return jax.shard_map(body, mesh=mesh, in_specs=in_specs, out_specs=out_specs, check_vma=False)
```
